32 devices in a mesh: expert: 16 (over z, y, x), half: 2 (over core).
Axes of the slice: x: 2, y: 2, z: 4, core: 2. Of those that a mesh axis runs over, the one named last changes fastest.
Arguments:
- tokens: bfloat16 [1024, 2048], P('expert'), may hold values from -6 to 6
- cotangent: bfloat16 [1024, 2048], P('expert'), may hold values from -1 to 1
- expert_ids: int32 [1024, 8], P('expert'), may hold values from 0 to 15, all different within a row; in each aligned block of 64 rows (0 to 63, 64 to 127, ...) at most 48 rows name the same one
- gate_weights: float32 [1024, 8], P('expert'), may hold values from 0.1 to 0.6
- w_gate: bfloat16 [16, 2048, 768], P('expert', None, 'half'), may hold values from -0.125 to 0.125
- w_up: bfloat16 [16, 2048, 768], P('expert', None, 'half'), may hold values from -0.125 to 0.125
- w_down: bfloat16 [16, 768, 2048], P('expert', 'half'), may hold values from -0.21875 to 0.21875
Outputs:
- input_grad: bfloat16 [1024, 2048], P('expert')
- gate_grad: bfloat16 [1024, 8], P('expert')
The draws below stay inside these ranges and needn't reach their ends.
Inputs may be any that keep to these rules, and one draw needn't show every extreme that they name: `expert_ids`: each token names 8 different experts. Among the 64 tokens of one index of expert, no expert is named by more than 48 tokens, a bound that some block reaches; every expert is named somewhere.
All inputs are finite; a program needn't handle non-finite values.
Results may differ from the reference program's by a relative error of at most 0.0085.
Values may be sent and summed in bfloat16 or wider, within the bound.
No kernel may reach another device: no remote copies, remote signals or barrier semaphores. Data moves between devices by JAX's collectives and lax.ppermute only.
A program may use at most 64 MiB of HBM per device.

```python
import math
import jax
import jax.numpy as jnp
import numpy as np
from jax import lax

D = 2048
FF = 768
TOP = 8
TOK_DEV = 64
EXPERTS = 16
CAP = 48
TOKENS = 1024
N_EXPERT = 16


def level_of(rng, extent, cuts, smallest, high):
    def one(dim, parts):
        steps = jax.random.uniform(jax.random.fold_in(jax.random.fold_in(rng, 6), dim), (parts,), jnp.float32, smallest / len(cuts), high / len(cuts))
        return jnp.repeat(jnp.exp(steps), extent[dim] // parts).reshape((-1,) + (1,) * (len(extent) - dim - 1))

    factor_of = one(*cuts[0])
    for cut in cuts[1:]:
        factor_of = factor_of * one(*cut)
    return factor_of


def routed_block(stream_key, own, number, rows, number_of, top, most, lean):
    sequence = jax.random.permutation(stream_key, number_of)
    packed, ordinary = portions_of(number_of, rows * top, most, lean, True), portions_of(number_of, rows * top, most, lean, False)
    places = jnp.arange(number_of)

    def named(sizes, offset_by):
        used = int((sizes > 0).sum())
        fixed = max(1, used // 4)
        passed = fixed + (places - fixed + offset_by * (used - fixed)) % max(1, number_of - fixed)
        return jnp.zeros((number_of,), jnp.int32).at[sequence[jnp.where(places < fixed, places, passed)]].set(jnp.asarray(sizes, jnp.int32))

    sizes = jnp.where(number % 4 == 0, named(packed, number // 4), named(ordinary, number - number // 4 - 1))
    mixed = jax.random.permutation(jax.random.fold_in(own, 3), number_of)
    donor, receiver = mixed[0:number_of // 2 * 2:2], mixed[1:number_of // 2 * 2:2]
    margin = jnp.minimum(sizes[donor] - 1, most - sizes[receiver]) // 2
    margin = jnp.where((donor == sequence[0]) | (receiver == sequence[0]) | (sizes[receiver] == 0), 0, jnp.maximum(margin, 0))
    passed = jax.random.randint(jax.random.fold_in(own, 4), (number_of // 2,), 0, 1 << 20) % (margin + 1)
    sizes = sizes.at[donor].add(-passed).at[receiver].add(passed)
    items = jnp.searchsorted(jnp.cumsum(sizes), jnp.arange(rows * top), side="right").astype(jnp.int32)
    listing = items.reshape(top, rows).T
    listing = listing[jax.random.permutation(jax.random.fold_in(own, 1), rows)]
    offset_by = jax.random.randint(jax.random.fold_in(own, 2), (rows, 1), 0, top)
    return jnp.take_along_axis(listing, (jnp.arange(top)[None, :] + offset_by) % top, axis=1)


def portions_of(amount, total, bound, lean, full):
    loads = [(1 << 20) // math.isqrt(standing ** lean) + 1 for standing in range(1, amount + 1)]
    largest = bound if full else min(bound, max(-(-total // amount), total * loads[0] // sum(loads)))
    least = 1 if total - largest >= amount - 1 else 0
    holding, rest = [largest] + [least] * (amount - 1), total - largest - least * (amount - 1)
    while rest > 0:
        candidates = [i for i in range(1, amount) if holding[i] < largest] or [i for i in range(1, amount) if holding[i] < bound]
        pool, remaining = sum([loads[i] for i in candidates]), rest
        for i in candidates:
            addition = min(bound - holding[i], max(1, remaining * loads[i] // pool), rest)
            holding[i] = holding[i] + addition
            rest = rest - addition
    return np.array(holding)


def scatter_about(own_key, extent, scale, bound, split=(), kind=jnp.bfloat16):
    factor_of = level_of(own_key, extent, split, -0.22, 0.18) if split else 1.0
    array = jax.random.normal(own_key, extent, jnp.float32) * scale * factor_of
    return jnp.minimum(jnp.maximum(array, -bound), bound).astype(kind)


def setup_inputs(seed: int = 0) -> dict:
    keys = jax.random.split(jax.random.key(seed), 8)
    tokens = scatter_about(keys[0], (TOKENS, D), 1.0, 6.0, ((0, 16),))
    cotangent = scatter_about(keys[1], (TOKENS, D), 0.15, 1.0, ((0, 16),))
    expert_ids_keys = jax.random.split(jax.random.fold_in(keys[2], 1), TOKENS // TOK_DEV)
    expert_ids_turns = jax.random.permutation(jax.random.fold_in(keys[2], 3), TOKENS // TOK_DEV)
    expert_ids = jax.vmap(lambda own, number: routed_block(jax.random.fold_in(keys[2], 2), own, number, TOK_DEV, EXPERTS, TOP, CAP, 2))(expert_ids_keys, expert_ids_turns).reshape((TOKENS, TOP))
    gate_weights = jnp.clip(0.1 + 0.5 * jax.random.uniform(keys[3], (TOKENS, TOP), jnp.float32) ** level_of(keys[3], (TOKENS, TOP), ((0, 16),), -0.2, 0.2), 0.1, 0.6)
    w_gate = scatter_about(keys[4], (EXPERTS, D, FF), D ** -0.5, 0.125, ((0, 16), (2, 2)))
    w_up = scatter_about(keys[5], (EXPERTS, D, FF), D ** -0.5, 0.125, ((0, 16), (2, 2)))
    w_down = scatter_about(keys[6], (EXPERTS, FF, D), FF ** -0.5, 0.21875, ((0, 16), (1, 2)))
    return dict(tokens=tokens, cotangent=cotangent, expert_ids=expert_ids, gate_weights=gate_weights, w_gate=w_gate, w_up=w_up, w_down=w_down)


def expert_terms(rows, grads, gate_one, up_one, down_one):
    gate_pre = jnp.dot(rows, gate_one, preferred_element_type=jnp.float32)
    up_pre = jnp.dot(rows, up_one, preferred_element_type=jnp.float32)
    grad_hidden = jnp.dot(grads, down_one.T, preferred_element_type=jnp.float32)
    sigmoid_gate = jax.nn.sigmoid(gate_pre)
    silu_gate = gate_pre * sigmoid_gate
    scores = jnp.sum(grad_hidden * silu_gate * up_pre, axis=-1)
    grad_up = (grad_hidden * silu_gate).astype(jnp.bfloat16)
    grad_gate = (grad_hidden * up_pre * sigmoid_gate * (1.0 + gate_pre * (1.0 - sigmoid_gate))).astype(jnp.bfloat16)
    input_part = jnp.dot(grad_gate, gate_one.T, preferred_element_type=jnp.float32)
    input_part = input_part + jnp.dot(grad_up, up_one.T, preferred_element_type=jnp.float32)
    return input_part, scores


def reference(tokens, cotangent, expert_ids, gate_weights, w_gate, w_up, w_down):
    tok_total = tokens.shape[0]
    routed = expert_ids.reshape(-1).astype(jnp.int32)
    pair_total = routed.shape[0]
    order = jnp.argsort(routed, stable=True).astype(jnp.int32)
    counts = jnp.bincount(routed, length=EXPERTS).astype(jnp.int32)
    starts = (jnp.cumsum(counts) - counts).astype(jnp.int32)
    most = N_EXPERT * CAP
    gates_flat = gate_weights.reshape(-1)

    def visit(totals, expert):
        input_sum, gate_sum = totals
        offsets = jnp.arange(most, dtype=jnp.int32)
        slot_live = offsets < counts[expert]
        pairs = order[jnp.minimum(starts[expert] + offsets, pair_total - 1)].astype(jnp.int32)
        owners = (pairs // TOP).astype(jnp.int32)
        rows = jnp.where(slot_live[:, None], tokens[owners], jnp.zeros((), tokens.dtype))
        grads = jnp.where(slot_live[:, None], cotangent[owners], jnp.zeros((), cotangent.dtype))
        input_part, scores = expert_terms(rows, grads, w_gate[expert], w_up[expert], w_down[expert])
        rounded = lax.optimization_barrier(input_part.astype(jnp.bfloat16)).astype(jnp.float32)
        weighted = jnp.where(slot_live[:, None], gates_flat[pairs][:, None] * rounded, jnp.zeros((), jnp.float32))
        input_sum = input_sum.at[owners].add(weighted)
        gate_sum = gate_sum.at[pairs].add(jnp.where(slot_live, scores, jnp.zeros((), jnp.float32)))
        return (input_sum, gate_sum), None

    start_state = (jnp.zeros((tok_total, D), jnp.float32), jnp.zeros((pair_total,), jnp.float32))
    (input_sum, gate_sum), unused = lax.scan(visit, start_state, jnp.arange(EXPERTS, dtype=jnp.int32))
    return input_sum.astype(jnp.bfloat16), gate_sum.reshape(tok_total, TOP).astype(jnp.bfloat16)
```

```python
import functools

import jax
import jax.numpy as jnp
from jax import lax
from jax.experimental import pallas as pl
from jax.experimental.pallas import tpu as pltpu
from jax.sharding import PartitionSpec as P

LANES = 128


def expert_terms(rows, grads, gate_one, up_one, down_one):
    gate_pre = jnp.einsum("ncd,df->ncf", rows, gate_one, preferred_element_type=jnp.float32)
    up_pre = jnp.einsum("ncd,df->ncf", rows, up_one, preferred_element_type=jnp.float32)
    grad_hidden = jnp.einsum("ncd,fd->ncf", grads, down_one, preferred_element_type=jnp.float32)
    sigmoid_gate = jax.nn.sigmoid(gate_pre)
    silu_gate = gate_pre * sigmoid_gate
    scores = jnp.sum(grad_hidden * silu_gate * up_pre, axis=-1)
    grad_up = (grad_hidden * silu_gate).astype(jnp.bfloat16)
    grad_gate = (
        grad_hidden * up_pre * sigmoid_gate * (1.0 + gate_pre * (1.0 - sigmoid_gate))
    ).astype(jnp.bfloat16)
    input_part = jnp.einsum("ncf,df->ncd", grad_gate, gate_one, preferred_element_type=jnp.float32)
    input_part = input_part + jnp.einsum(
        "ncf,df->ncd", grad_up, up_one, preferred_element_type=jnp.float32
    )
    return (input_part, scores)


def owner_sum(back, slot_index, gate_weights):
    width = back.shape[2]
    picked = back.reshape(-1, width)[slot_index]
    picked = picked.reshape(gate_weights.shape[0], gate_weights.shape[1], width)
    return jnp.einsum(
        "tk,tkw->tw", gate_weights, picked, preferred_element_type=jnp.float32
    ).astype(jnp.bfloat16)


def routed_plan(tokens, cotangent, expert_ids, gate_weights, w_gate, w_up, w_down):
    tok_count, top_count = expert_ids.shape
    experts = lax.axis_size("expert")
    capacity = 3 * tok_count * top_count // (2 * experts)
    routed = expert_ids.reshape(-1)
    onehot = (routed[:, None] == jnp.arange(experts, dtype=jnp.int32)[None, :]).astype(jnp.int32)
    earlier = jnp.cumsum(onehot, axis=0) - onehot
    slot_index = routed * capacity + jnp.sum(earlier * onehot, axis=1)
    owner_rows = jnp.arange(tok_count * top_count, dtype=jnp.int32) // top_count + 1
    slot_token = jnp.zeros((experts * capacity,), jnp.int32).at[slot_index].set(owner_rows)
    slot_live = (slot_token > 0)[:, None]
    picked = jnp.maximum(slot_token - 1, 0)
    sent_tokens = jnp.where(slot_live, tokens[picked], jnp.zeros((), tokens.dtype)).reshape(
        experts, capacity, -1
    )
    sent_grads = jnp.where(slot_live, cotangent[picked], jnp.zeros((), cotangent.dtype)).reshape(
        experts, capacity, -1
    )
    gate_one = w_gate[0]
    up_one = w_up[0]
    down_one = w_down[0]
    gate_full, up_full = (
        lax.all_gather(gate_one, "half", axis=1, tiled=True),
        lax.all_gather(up_one, "half", axis=1, tiled=True),
    )
    down_full = lax.all_gather(down_one, "half", axis=0, tiled=True)
    half_slots = capacity // 2
    first_slot = lax.axis_index("half") * half_slots
    own_tokens = lax.dynamic_slice_in_dim(sent_tokens, first_slot, half_slots, 1)
    own_grads = lax.dynamic_slice_in_dim(sent_grads, first_slot, half_slots, 1)
    rows = lax.all_to_all(own_tokens, "expert", split_axis=0, concat_axis=0, tiled=True)
    grads = lax.all_to_all(own_grads, "expert", split_axis=0, concat_axis=0, tiled=True)
    part, score = expert_terms(rows, grads, gate_full, up_full, down_full)
    slot_part = part.astype(jnp.bfloat16)
    slot_scores = score.astype(jnp.bfloat16)
    back_part, back_part_scores = (
        lax.all_to_all(slot_part, "expert", split_axis=0, concat_axis=0, tiled=True),
        lax.all_to_all(slot_scores, "expert", split_axis=0, concat_axis=0, tiled=True),
    )
    back, back_scores = (
        lax.all_gather(back_part, "half", axis=1, tiled=True),
        lax.all_gather(back_part_scores, "half", axis=1, tiled=True),
    )
    input_grad = owner_sum(back, slot_index, gate_weights)
    gate_grad = back_scores.reshape(-1)[slot_index].reshape(tok_count, top_count)
    return (input_grad, gate_grad)


def padded(count):
    return -(-count // LANES) * LANES


def pack_kernel(experts, half_ref, tok_ref, cot_ref, ids_ref, gw_ref, out_ref):
    rows, width = tok_ref.shape
    out_ref[:, 0:width] = tok_ref[...]
    out_ref[:, width : 2 * width] = cot_ref[...]
    lane = lax.broadcasted_iota(jnp.int32, (rows, out_ref.shape[1] - 2 * width), 1)
    total = jnp.zeros(lane.shape, jnp.float32)
    weights = gw_ref[...]
    high = weights.astype(jnp.bfloat16).astype(jnp.float32)
    low = weights - high
    ids = ids_ref[...]
    for k in range(ids.shape[1]):
        one = ids[:, k : k + 1]
        total = jnp.where(lane == one, high[:, k : k + 1], total)
        total = jnp.where(lane == one + experts, low[:, k : k + 1], total)
    out_ref[:, 2 * width :] = total.astype(jnp.bfloat16)


def pack(half, tokens, cotangent, expert_ids, gate_weights, experts):
    tok_count, width = tokens.shape
    rows, top = tok_count // 2, expert_ids.shape[1]
    own = lambda i, half: (half[0], 0)
    return pl.pallas_call(
        functools.partial(pack_kernel, experts),
        grid_spec=pltpu.PrefetchScalarGridSpec(
            num_scalar_prefetch=1,
            grid=(1,),
            in_specs=[
                pl.BlockSpec((rows, width), own),
                pl.BlockSpec((rows, width), own),
                pl.BlockSpec((rows, top), own),
                pl.BlockSpec((rows, top), own),
            ],
            out_specs=pl.BlockSpec((rows, 2 * width + padded(2 * experts)), lambda i, half: (0, 0)),
        ),
        out_shape=jax.ShapeDtypeStruct((rows, 2 * width + padded(2 * experts)), jnp.bfloat16),
        name="pack",
    )(half, tokens, cotangent, expert_ids, gate_weights)


def expert_kernel(experts, expert_ref, own_ref, first_ref, rest_ref, gate_up_ref, down_ref, near_ref, far_ref):
    rows = own_ref.shape[0]
    width, units = gate_up_ref.shape[0], down_ref.shape[0]
    contract_last = (((1,), (1,)), ((), ()))
    packed = jnp.concatenate([own_ref[...], first_ref[...], rest_ref[...]], axis=0)
    pre = jnp.dot(packed[:, :width], gate_up_ref[...], preferred_element_type=jnp.float32)
    grad_hidden = lax.dot_general(
        packed[:, width : 2 * width], down_ref[...], contract_last, preferred_element_type=jnp.float32
    )
    gate_pre, up_pre = pre[:, :units], pre[:, units:]
    sigmoid_gate = 1.0 / (1.0 + jnp.exp(-gate_pre))
    grad_up = grad_hidden * gate_pre * sigmoid_gate
    scores = jnp.sum(grad_up * up_pre, axis=1, keepdims=True)
    grad_gate = grad_hidden * up_pre * sigmoid_gate * (1.0 + gate_pre * (1.0 - sigmoid_gate))
    grads = jnp.concatenate([grad_gate.astype(jnp.bfloat16), grad_up.astype(jnp.bfloat16)], axis=1)
    part = lax.dot_general(grads, gate_up_ref[...], contract_last, preferred_element_type=jnp.float32)
    expert = expert_ref[0]
    routing = packed[:, 2 * width :].astype(jnp.float32)
    lane = lax.broadcasted_iota(jnp.int32, routing.shape, 1)
    weight = jnp.sum(
        jnp.where((lane == expert) | (lane == expert + experts), routing, 0.0), axis=1, keepdims=True
    )
    part = (part * weight).astype(jnp.bfloat16)
    columns = near_ref.shape[1] - width
    column = lax.broadcasted_iota(jnp.int32, (packed.shape[0], columns), 1)
    score_part = jnp.where(column == expert, scores, 0.0).astype(jnp.bfloat16)
    near_ref[:, :width] = part[: 2 * rows]
    near_ref[:, width:] = score_part[: 2 * rows]
    far_ref[:, :width] = part[2 * rows :]
    far_ref[:, width:] = score_part[2 * rows :]


def expert_call(expert, own, first, rest, gate_up, down, experts):
    rows = own.shape[0]
    width, units = gate_up.shape[0], down.shape[0]
    out = jax.ShapeDtypeStruct((2 * rows, width + padded(experts)), jnp.bfloat16)
    vmem = pl.BlockSpec(memory_space=pltpu.VMEM)
    return pl.pallas_call(
        functools.partial(expert_kernel, experts),
        in_specs=[pl.BlockSpec(memory_space=pltpu.SMEM)] + [vmem] * 5,
        out_specs=(vmem, vmem),
        out_shape=(out, out),
        compiler_params=pltpu.CompilerParams(vmem_limit_bytes=40 * 2**20),
        cost_estimate=pl.CostEstimate(
            flops=2 * 4 * rows * width * units * 5, bytes_accessed=gate_up.size * 3, transcendentals=0
        ),
        name="expert",
    )(expert, own, first, rest, gate_up, down)


def finish_kernel(half_ref, own_ref, other_ref, ids_ref, grad_ref, score_ref):
    rows, width = own_ref.shape[0], grad_ref.shape[1]
    half = half_ref[0]
    for ref, place in ((own_ref, half), (other_ref, 1 - half)):
        block = pl.ds(pl.multiple_of(place * rows, rows), rows)
        grad_ref[block, :] = ref[:, :width]
        scores = ref[:, width:].astype(jnp.float32)
        column = lax.broadcasted_iota(jnp.int32, scores.shape, 1)
        ids = ids_ref[block, :]
        place_of = lax.broadcasted_iota(jnp.int32, ids.shape, 1)
        total = jnp.zeros(ids.shape, jnp.float32)
        for k in range(ids.shape[1]):
            one = jnp.sum(jnp.where(column == ids[:, k : k + 1], scores, 0.0), axis=1, keepdims=True)
            total = jnp.where(place_of == k, one, total)
        score_ref[block, :] = total


def finish(half, own, other, expert_ids, width):
    vmem = pl.BlockSpec(memory_space=pltpu.VMEM)
    grad, score = pl.pallas_call(
        finish_kernel,
        in_specs=[pl.BlockSpec(memory_space=pltpu.SMEM)] + [vmem] * 3,
        out_specs=(vmem, vmem),
        out_shape=(
            jax.ShapeDtypeStruct((expert_ids.shape[0], width), jnp.bfloat16),
            jax.ShapeDtypeStruct(expert_ids.shape, jnp.float32),
        ),
        name="finish",
    )(half, own, other, expert_ids)
    return grad, score.astype(jnp.bfloat16)


def added(*terms):
    total = terms[0].astype(jnp.float32)
    for term in terms[1:]:
        total = total + term.astype(jnp.float32)
    return total.astype(jnp.bfloat16)


def dense_plan(tokens, cotangent, expert_ids, gate_weights, w_gate, w_up, w_down):
    experts, halves = lax.axis_size("expert"), lax.axis_size("half")
    levels = experts // 4
    width = tokens.shape[1]
    rows = tokens.shape[0] // 2
    half = lax.axis_index("half").reshape(1).astype(jnp.int32)
    expert = lax.axis_index("expert").reshape(1).astype(jnp.int32)
    axes = ("expert", "half")

    first_pairs = [(e * 2 + h, (e ^ (1 + h)) * 2 + h) for e in range(experts) for h in range(halves)]
    second_pairs = [(e * 2 + h, (e ^ (2 - h)) * 2 + h) for e in range(experts) for h in range(halves)]
    ring_pairs = [(e, (e + 4) % experts) for e in range(experts)]
    swap_pairs = [(0, 1), (1, 0)]
    to_first = lambda a: lax.ppermute(a, axes, first_pairs)
    to_second = lambda a: lax.ppermute(a, axes, second_pairs)
    along_ring = lambda a: lax.ppermute(a, "expert", ring_pairs)
    swapped = lambda a: lax.ppermute(a, "half", swap_pairs)

    own = pack(half, tokens, cotangent, expert_ids, gate_weights, experts)
    gate_one, up_one, down_one = w_gate[0], w_up[0], w_down[0]
    gate_up = jnp.concatenate([gate_one, swapped(gate_one), up_one, swapped(up_one)], axis=1)
    down = jnp.concatenate([down_one, swapped(down_one)], axis=0)

    planes = []
    shard = own
    for level in range(levels):
        first = to_first(shard)
        rest = to_second(jnp.concatenate([shard, first], axis=0))
        planes.append((shard, first, rest))
        if level < levels - 1:
            shard = along_ring(shard)

    sums = []
    for shard, first, rest in planes:
        near, far = expert_call(expert, shard, first, rest, gate_up, down, experts)
        from_second = to_second(far)
        from_first = to_first(added(near[rows:], from_second[rows:]))
        sums.append((near[:rows], from_second[:rows], from_first))
    carry = None
    for level in list(range(1, levels)) + [0]:
        terms = sums[level] if carry is None else sums[level] + (carry,)
        carry = added(*terms)
        if level:
            carry = along_ring(carry)
    return finish(half, carry, swapped(carry), expert_ids, width)


def solution(mesh):
    placed = (
        P("expert", None),
        P("expert", None),
        P("expert", None),
        P("expert", None),
        P("expert", None, "half"),
        P("expert", None, "half"),
        P("expert", "half", None),
    )

    def per_device(tokens, cotangent, expert_ids, *others):
        experts, top = mesh.shape["expert"], expert_ids.shape[1]
        dense = experts <= 2 * top and experts % 4 == 0 and mesh.shape["half"] == 2
        return (dense_plan if dense else routed_plan)(tokens, cotangent, expert_ids, *others)

    return jax.shard_map(
        per_device,
        mesh=mesh,
        in_specs=placed,
        out_specs=(P("expert", None), P("expert", None)),
        check_vma=False,
    )
```

```python
import functools

import jax
import jax.numpy as jnp
from jax import lax
from jax.experimental import pallas as pl
from jax.experimental.pallas import tpu as pltpu
from jax.sharding import PartitionSpec as P

LANES = 128
LAG = 10000000000
EFLOPS = 5000000000
CONTRACT_LAST = (((1,), (1,)), ((), ()))


def expert_terms(rows, grads, gate_one, up_one, down_one):
    gate_pre = jnp.einsum("ncd,df->ncf", rows, gate_one, preferred_element_type=jnp.float32)
    up_pre = jnp.einsum("ncd,df->ncf", rows, up_one, preferred_element_type=jnp.float32)
    grad_hidden = jnp.einsum("ncd,fd->ncf", grads, down_one, preferred_element_type=jnp.float32)
    sigmoid_gate = jax.nn.sigmoid(gate_pre)
    silu_gate = gate_pre * sigmoid_gate
    scores = jnp.sum(grad_hidden * silu_gate * up_pre, axis=-1)
    grad_up = (grad_hidden * silu_gate).astype(jnp.bfloat16)
    grad_gate = (
        grad_hidden * up_pre * sigmoid_gate * (1.0 + gate_pre * (1.0 - sigmoid_gate))
    ).astype(jnp.bfloat16)
    input_part = jnp.einsum("ncf,df->ncd", grad_gate, gate_one, preferred_element_type=jnp.float32)
    input_part = input_part + jnp.einsum(
        "ncf,df->ncd", grad_up, up_one, preferred_element_type=jnp.float32
    )
    return (input_part, scores)


def owner_sum(back, slot_index, gate_weights):
    width = back.shape[2]
    picked = back.reshape(-1, width)[slot_index]
    picked = picked.reshape(gate_weights.shape[0], gate_weights.shape[1], width)
    return jnp.einsum(
        "tk,tkw->tw", gate_weights, picked, preferred_element_type=jnp.float32
    ).astype(jnp.bfloat16)


def routed_plan(tokens, cotangent, expert_ids, gate_weights, w_gate, w_up, w_down):
    tok_count, top_count = expert_ids.shape
    experts = lax.axis_size("expert")
    capacity = 3 * tok_count * top_count // (2 * experts)
    routed = expert_ids.reshape(-1)
    onehot = (routed[:, None] == jnp.arange(experts, dtype=jnp.int32)[None, :]).astype(jnp.int32)
    earlier = jnp.cumsum(onehot, axis=0) - onehot
    slot_index = routed * capacity + jnp.sum(earlier * onehot, axis=1)
    owner_rows = jnp.arange(tok_count * top_count, dtype=jnp.int32) // top_count + 1
    slot_token = jnp.zeros((experts * capacity,), jnp.int32).at[slot_index].set(owner_rows)
    slot_live = (slot_token > 0)[:, None]
    picked = jnp.maximum(slot_token - 1, 0)
    sent_tokens = jnp.where(slot_live, tokens[picked], jnp.zeros((), tokens.dtype)).reshape(
        experts, capacity, -1
    )
    sent_grads = jnp.where(slot_live, cotangent[picked], jnp.zeros((), cotangent.dtype)).reshape(
        experts, capacity, -1
    )
    gate_one = w_gate[0]
    up_one = w_up[0]
    down_one = w_down[0]
    gate_full, up_full = (
        lax.all_gather(gate_one, "half", axis=1, tiled=True),
        lax.all_gather(up_one, "half", axis=1, tiled=True),
    )
    down_full = lax.all_gather(down_one, "half", axis=0, tiled=True)
    half_slots = capacity // 2
    first_slot = lax.axis_index("half") * half_slots
    own_tokens = lax.dynamic_slice_in_dim(sent_tokens, first_slot, half_slots, 1)
    own_grads = lax.dynamic_slice_in_dim(sent_grads, first_slot, half_slots, 1)
    rows = lax.all_to_all(own_tokens, "expert", split_axis=0, concat_axis=0, tiled=True)
    grads = lax.all_to_all(own_grads, "expert", split_axis=0, concat_axis=0, tiled=True)
    part, score = expert_terms(rows, grads, gate_full, up_full, down_full)
    slot_part = part.astype(jnp.bfloat16)
    slot_scores = score.astype(jnp.bfloat16)
    back_part, back_part_scores = (
        lax.all_to_all(slot_part, "expert", split_axis=0, concat_axis=0, tiled=True),
        lax.all_to_all(slot_scores, "expert", split_axis=0, concat_axis=0, tiled=True),
    )
    back, back_scores = (
        lax.all_gather(back_part, "half", axis=1, tiled=True),
        lax.all_gather(back_part_scores, "half", axis=1, tiled=True),
    )
    input_grad = owner_sum(back, slot_index, gate_weights)
    gate_grad = back_scores.reshape(-1)[slot_index].reshape(tok_count, top_count)
    return (input_grad, gate_grad)


def padded(count):
    return -(-count // LANES) * LANES


def pack_kernel(experts, half_ref, tok_ref, cot_ref, ids_ref, gw_ref, out_ref):
    rows, width = tok_ref.shape
    out_ref[:, 0:width] = tok_ref[...]
    out_ref[:, width : 2 * width] = cot_ref[...]
    top, count = ids_ref.shape
    slot = lax.broadcasted_iota(jnp.int32, (out_ref.shape[1] - 2 * width, count), 0)
    total = jnp.zeros(slot.shape, jnp.float32)
    for k in range(top):
        one, weight = ids_ref[k : k + 1, :], gw_ref[k : k + 1, :]
        high = weight.astype(jnp.bfloat16).astype(jnp.float32)
        total = jnp.where(slot == one, high, total)
        total = jnp.where(slot == one + experts, weight - high, total)
    row = lax.broadcasted_iota(jnp.int32, (rows, count), 0) + half_ref[0] * rows
    pick = (row == lax.broadcasted_iota(jnp.int32, (rows, count), 1)).astype(jnp.bfloat16)
    out_ref[:, 2 * width :] = lax.dot_general(
        pick, total.astype(jnp.bfloat16), CONTRACT_LAST, preferred_element_type=jnp.float32
    ).astype(jnp.bfloat16)


def pack(half, tokens, cotangent, expert_ids, gate_weights, experts):
    tok_count, width = tokens.shape
    rows, top = tok_count // 2, expert_ids.shape[1]
    own = lambda i, half: (half[0], 0)
    whole = lambda i, half: (0, 0)
    return pl.pallas_call(
        functools.partial(pack_kernel, experts),
        grid_spec=pltpu.PrefetchScalarGridSpec(
            num_scalar_prefetch=1,
            grid=(1,),
            in_specs=[
                pl.BlockSpec((rows, width), own),
                pl.BlockSpec((rows, width), own),
                pl.BlockSpec((top, tok_count), whole),
                pl.BlockSpec((top, tok_count), whole),
            ],
            out_specs=pl.BlockSpec((rows, 2 * width + padded(2 * experts)), whole),
        ),
        out_shape=jax.ShapeDtypeStruct((rows, 2 * width + padded(2 * experts)), jnp.bfloat16),
        name="pack",
    )(half, tokens, cotangent, expert_ids.T, gate_weights.T)


def expert_kernel(experts, expert_ref, gate_up_ref, down_ref, *refs):
    shard_refs, out_refs = refs[: 2 * len(refs) // 3], refs[2 * len(refs) // 3 :]
    rows = 2 * shard_refs[0].shape[0]
    width, units = gate_up_ref.shape[0], down_ref.shape[0]
    packed = jnp.concatenate([ref[...] for ref in shard_refs], axis=0)
    pre = jnp.dot(packed[:, :width], gate_up_ref[...], preferred_element_type=jnp.float32)
    grad_hidden = lax.dot_general(
        packed[:, width : 2 * width], down_ref[...], CONTRACT_LAST, preferred_element_type=jnp.float32
    )
    gate_pre, up_pre = pre[:, :units], pre[:, units:]
    sigmoid_gate = 1.0 / (1.0 + jnp.exp(-gate_pre))
    grad_up = grad_hidden * gate_pre * sigmoid_gate
    scores = jnp.sum(grad_up * up_pre, axis=1, keepdims=True)
    grad_gate = grad_hidden * up_pre * sigmoid_gate * (1.0 + gate_pre * (1.0 - sigmoid_gate))
    grads = jnp.concatenate([grad_gate.astype(jnp.bfloat16), grad_up.astype(jnp.bfloat16)], axis=1)
    part = lax.dot_general(grads, gate_up_ref[...], CONTRACT_LAST, preferred_element_type=jnp.float32)
    expert = expert_ref[0]
    routing = packed[:, 2 * width :].astype(jnp.float32)
    lane = lax.broadcasted_iota(jnp.int32, routing.shape, 1)
    weight = jnp.sum(
        jnp.where((lane == expert) | (lane == expert + experts), routing, 0.0), axis=1, keepdims=True
    )
    part = (part * weight).astype(jnp.bfloat16)
    column = lax.broadcasted_iota(jnp.int32, (packed.shape[0], out_refs[0].shape[1] - width), 1)
    score_part = jnp.where(column == expert, scores, 0.0).astype(jnp.bfloat16)
    for i, ref in enumerate(out_refs):
        ref[:, :width] = part[i * rows : (i + 1) * rows]
        ref[:, width:] = score_part[i * rows : (i + 1) * rows]


def expert_call(expert, gate_up, down, experts, *shards):
    rows = shards[0].shape[0]
    width, units = gate_up.shape[0], down.shape[0]
    outs = len(shards) // 2
    vmem = pl.BlockSpec(memory_space=pltpu.VMEM)
    return pl.pallas_call(
        functools.partial(expert_kernel, experts),
        in_specs=[pl.BlockSpec(memory_space=pltpu.SMEM)] + [vmem] * (2 + len(shards)),
        out_specs=[vmem] * outs,
        out_shape=[jax.ShapeDtypeStruct((2 * rows, width + padded(experts)), jnp.bfloat16)] * outs,
        compiler_params=pltpu.CompilerParams(vmem_limit_bytes=40 * 2**20),
        cost_estimate=pl.CostEstimate(flops=EFLOPS, bytes_accessed=1, transcendentals=0),
        name="expert",
    )(expert, gate_up, down, *shards)


def tie(*arrays, cost=1):
    return pl.pallas_call(
        lambda *refs: None,
        in_specs=[pl.BlockSpec(memory_space=pl.ANY)] * len(arrays),
        out_specs=[pl.BlockSpec(memory_space=pl.ANY)] * len(arrays),
        out_shape=[jax.ShapeDtypeStruct(a.shape, a.dtype) for a in arrays],
        input_output_aliases={i: i for i in range(len(arrays))},
        compiler_params=pltpu.CompilerParams(vmem_limit_bytes=2**18),
        cost_estimate=pl.CostEstimate(flops=cost, bytes_accessed=1, transcendentals=0),
        name="tie",
    )(*arrays)


def finish_kernel(half_ref, own_ref, other_ref, ids_ref, grad_ref, score_ref):
    rows, width = own_ref.shape[0], grad_ref.shape[1]
    half = half_ref[0]
    columns = own_ref.shape[1] - width
    pair = lax.broadcasted_iota(jnp.int32, (columns, columns), 0)
    same = (pair == lax.broadcasted_iota(jnp.int32, (columns, columns), 1)).astype(jnp.bfloat16)
    scores = jnp.zeros((columns, 2 * rows), jnp.float32)
    for ref, place in ((own_ref, half), (other_ref, 1 - half)):
        grad_ref[pl.ds(pl.multiple_of(place * rows, rows), rows), :] = ref[:, :width]
        row = lax.broadcasted_iota(jnp.int32, (2 * rows, rows), 0) - place * rows
        spot = (row == lax.broadcasted_iota(jnp.int32, (2 * rows, rows), 1)).astype(jnp.bfloat16)
        turned = lax.dot_general(same, ref[:, width:], CONTRACT_LAST, preferred_element_type=jnp.float32)
        scores += lax.dot_general(
            turned.astype(jnp.bfloat16), spot, CONTRACT_LAST, preferred_element_type=jnp.float32
        )
    expert = lax.broadcasted_iota(jnp.int32, scores.shape, 0)
    place_of = lax.broadcasted_iota(jnp.int32, ids_ref.shape, 0)
    total = jnp.zeros(ids_ref.shape, jnp.float32)
    for k in range(ids_ref.shape[0]):
        one = jnp.sum(jnp.where(expert == ids_ref[k : k + 1, :], scores, 0.0), axis=0, keepdims=True)
        total = jnp.where(place_of == k, one, total)
    score_ref[...] = total.astype(jnp.bfloat16)


def finish(half, own, other, expert_ids, width):
    vmem = pl.BlockSpec(memory_space=pltpu.VMEM)
    grad, score = pl.pallas_call(
        finish_kernel,
        in_specs=[pl.BlockSpec(memory_space=pltpu.SMEM)] + [vmem] * 3,
        out_specs=(vmem, vmem),
        out_shape=(
            jax.ShapeDtypeStruct((expert_ids.shape[0], width), jnp.bfloat16),
            jax.ShapeDtypeStruct(expert_ids.shape[::-1], jnp.bfloat16),
        ),
        compiler_params=pltpu.CompilerParams(vmem_limit_bytes=4 * 2**20),
        name="finish",
    )(half, own, other, expert_ids.T)
    return grad, score.T


def added(*terms):
    total = terms[0].astype(jnp.float32)
    for term in terms[1:]:
        total = total + term.astype(jnp.float32)
    return total.astype(jnp.bfloat16)


def dense_plan(tokens, cotangent, expert_ids, gate_weights, w_gate, w_up, w_down):
    experts, halves = lax.axis_size("expert"), lax.axis_size("half")
    levels = experts // 4
    width = tokens.shape[1]
    rows = tokens.shape[0] // 2
    half = lax.axis_index("half").reshape(1).astype(jnp.int32)
    expert = lax.axis_index("expert").reshape(1).astype(jnp.int32)
    axes = ("expert", "half")

    first_pairs = [(e * 2 + h, (e ^ (1 + h)) * 2 + h) for e in range(experts) for h in range(halves)]
    second_pairs = [(e * 2 + h, (e ^ (2 - h)) * 2 + h) for e in range(experts) for h in range(halves)]
    swap_pairs = [(0, 1), (1, 0)]
    to_first = lambda a: lax.ppermute(a, axes, first_pairs)
    to_second = lambda a: lax.ppermute(a, axes, second_pairs)
    swapped = lambda a: lax.ppermute(a, "half", swap_pairs)

    own = pack(half, tokens, cotangent, expert_ids, gate_weights, experts)
    gate_one, up_one, down_one = w_gate[0], w_up[0], w_down[0]
    gate_up = jnp.concatenate([gate_one, swapped(gate_one), up_one, swapped(up_one)], axis=1)
    down = jnp.concatenate([down_one, swapped(down_one)], axis=0)

    shifted = lambda a, by: lax.ppermute(a, "expert", [(e, (e + 4 * by) % experts) for e in range(experts)])
    shards, firsts, seconds, boths = [own], [], [], []
    for level in range(levels):
        firsts.append(to_first(shards[level]))
        seconds.append(to_second(shards[level]))
        if level == levels - 1:
            boths.append(shifted(boths[0], level))
            break
        following = shifted(shards[level], 1)
        held = [following, firsts[level]]
        if level > 1:
            held += tie(seconds[level - 1], boths[level - 2], cost=LAG)
        elif level > 0:
            held.append(seconds[level - 1])
        if level == levels - 2:
            held += [gate_up, down]
        held = tie(*held)
        following, firsts[level] = held[:2]
        if level > 0:
            seconds[level - 1] = held[2]
        if level > 1:
            boths[level - 2] = held[3]
        if level == levels - 2:
            gate_up, down = held[-2:]
        shards.append(following)
        boths.append(to_second(firsts[level]))

    total, results, previous = [], {}, None
    for batch in ((1,0),(2,),(3,)):
        planes = [[shards[i], firsts[i], seconds[i], boths[i]] for i in batch]
        if previous is not None:
            results[previous][1], planes[0][0] = tie(results[previous][1], planes[0][0])
        outs = expert_call(expert, gate_up, down, experts, *sum(planes, []))
        for i, level in enumerate(batch):
            results[level] = list(outs[2 * i : 2 * i + 2])
        previous = batch[0]
    for level, (near, far) in results.items():
        from_second = to_second(far)
        from_first = to_first(added(near[rows:], from_second[rows:]))
        terms = (near[:rows], from_second[:rows], from_first)
        total += [shifted(added(*terms), levels - level)] if level else terms
    carry = added(*total)
    return finish(half, carry, swapped(carry), expert_ids, width)


def solution(mesh):
    placed = (
        P("expert", None),
        P("expert", None),
        P("expert", None),
        P("expert", None),
        P("expert", None, "half"),
        P("expert", None, "half"),
        P("expert", "half", None),
    )

    def per_device(tokens, cotangent, expert_ids, *others):
        experts, top = mesh.shape["expert"], expert_ids.shape[1]
        dense = 12 <= experts <= 2 * top and experts % 4 == 0 and mesh.shape["half"] == 2
        return (dense_plan if dense else routed_plan)(tokens, cotangent, expert_ids, *others)

    return jax.shard_map(
        per_device,
        mesh=mesh,
        in_specs=placed,
        out_specs=(P("expert", None), P("expert", None)),
        check_vma=False,
    )
```

```python
import functools

import jax
import jax.numpy as jnp
from jax import lax
from jax.experimental import pallas as pl
from jax.experimental.pallas import tpu as pltpu
from jax.sharding import PartitionSpec as P

LANES = 128
VM = 16
PREP = 4 * 10**9
LAG = 10000000000
EFLOPS = 5 * 10**9
CONTRACT_LAST = (((1,), (1,)), ((), ()))


def expert_terms(rows, grads, gate_one, up_one, down_one):
    gate_pre = jnp.einsum("ncd,df->ncf", rows, gate_one, preferred_element_type=jnp.float32)
    up_pre = jnp.einsum("ncd,df->ncf", rows, up_one, preferred_element_type=jnp.float32)
    grad_hidden = jnp.einsum("ncd,fd->ncf", grads, down_one, preferred_element_type=jnp.float32)
    sigmoid_gate = jax.nn.sigmoid(gate_pre)
    silu_gate = gate_pre * sigmoid_gate
    scores = jnp.sum(grad_hidden * silu_gate * up_pre, axis=-1)
    grad_up = (grad_hidden * silu_gate).astype(jnp.bfloat16)
    grad_gate = (
        grad_hidden * up_pre * sigmoid_gate * (1.0 + gate_pre * (1.0 - sigmoid_gate))
    ).astype(jnp.bfloat16)
    input_part = jnp.einsum("ncf,df->ncd", grad_gate, gate_one, preferred_element_type=jnp.float32)
    input_part = input_part + jnp.einsum(
        "ncf,df->ncd", grad_up, up_one, preferred_element_type=jnp.float32
    )
    return (input_part, scores)


def owner_sum(back, slot_index, gate_weights):
    width = back.shape[2]
    picked = back.reshape(-1, width)[slot_index]
    picked = picked.reshape(gate_weights.shape[0], gate_weights.shape[1], width)
    return jnp.einsum(
        "tk,tkw->tw", gate_weights, picked, preferred_element_type=jnp.float32
    ).astype(jnp.bfloat16)


def routed_plan(tokens, cotangent, expert_ids, gate_weights, w_gate, w_up, w_down):
    tok_count, top_count = expert_ids.shape
    experts = lax.axis_size("expert")
    capacity = 3 * tok_count * top_count // (2 * experts)
    routed = expert_ids.reshape(-1)
    onehot = (routed[:, None] == jnp.arange(experts, dtype=jnp.int32)[None, :]).astype(jnp.int32)
    earlier = jnp.cumsum(onehot, axis=0) - onehot
    slot_index = routed * capacity + jnp.sum(earlier * onehot, axis=1)
    owner_rows = jnp.arange(tok_count * top_count, dtype=jnp.int32) // top_count + 1
    slot_token = jnp.zeros((experts * capacity,), jnp.int32).at[slot_index].set(owner_rows)
    slot_live = (slot_token > 0)[:, None]
    picked = jnp.maximum(slot_token - 1, 0)
    sent_tokens = jnp.where(slot_live, tokens[picked], jnp.zeros((), tokens.dtype)).reshape(
        experts, capacity, -1
    )
    sent_grads = jnp.where(slot_live, cotangent[picked], jnp.zeros((), cotangent.dtype)).reshape(
        experts, capacity, -1
    )
    gate_one = w_gate[0]
    up_one = w_up[0]
    down_one = w_down[0]
    gate_full, up_full = (
        lax.all_gather(gate_one, "half", axis=1, tiled=True),
        lax.all_gather(up_one, "half", axis=1, tiled=True),
    )
    down_full = lax.all_gather(down_one, "half", axis=0, tiled=True)
    half_slots = capacity // 2
    first_slot = lax.axis_index("half") * half_slots
    own_tokens = lax.dynamic_slice_in_dim(sent_tokens, first_slot, half_slots, 1)
    own_grads = lax.dynamic_slice_in_dim(sent_grads, first_slot, half_slots, 1)
    rows = lax.all_to_all(own_tokens, "expert", split_axis=0, concat_axis=0, tiled=True)
    grads = lax.all_to_all(own_grads, "expert", split_axis=0, concat_axis=0, tiled=True)
    part, score = expert_terms(rows, grads, gate_full, up_full, down_full)
    slot_part = part.astype(jnp.bfloat16)
    slot_scores = score.astype(jnp.bfloat16)
    back_part, back_part_scores = (
        lax.all_to_all(slot_part, "expert", split_axis=0, concat_axis=0, tiled=True),
        lax.all_to_all(slot_scores, "expert", split_axis=0, concat_axis=0, tiled=True),
    )
    back, back_scores = (
        lax.all_gather(back_part, "half", axis=1, tiled=True),
        lax.all_gather(back_part_scores, "half", axis=1, tiled=True),
    )
    input_grad = owner_sum(back, slot_index, gate_weights)
    gate_grad = back_scores.reshape(-1)[slot_index].reshape(tok_count, top_count)
    return (input_grad, gate_grad)


def padded(count):
    return -(-count // LANES) * LANES


def pack_kernel(experts, half_ref, tok_ref, cot_ref, ids_ref, gw_ref, out_ref):
    rows, width = tok_ref.shape
    out_ref[:, 0:width] = tok_ref[...]
    out_ref[:, width : 2 * width] = cot_ref[...]
    top, count = ids_ref.shape
    slot = lax.broadcasted_iota(jnp.int32, (out_ref.shape[1] - 2 * width, count), 0)
    total = jnp.zeros(slot.shape, jnp.float32)
    for k in range(top):
        one, weight = ids_ref[k : k + 1, :], gw_ref[k : k + 1, :]
        high = weight.astype(jnp.bfloat16).astype(jnp.float32)
        total = jnp.where(slot == one, high, total)
        total = jnp.where(slot == one + experts, weight - high, total)
    row = lax.broadcasted_iota(jnp.int32, (rows, count), 0) + half_ref[0] * rows
    pick = (row == lax.broadcasted_iota(jnp.int32, (rows, count), 1)).astype(jnp.bfloat16)
    out_ref[:, 2 * width :] = lax.dot_general(
        pick, total.astype(jnp.bfloat16), CONTRACT_LAST, preferred_element_type=jnp.float32
    ).astype(jnp.bfloat16)


def pack(half, tokens, cotangent, expert_ids, gate_weights, experts):
    tok_count, width = tokens.shape
    rows, top = tok_count // 2, expert_ids.shape[1]
    own = lambda i, half: (half[0], 0)
    whole = lambda i, half: (0, 0)
    return pl.pallas_call(
        functools.partial(pack_kernel, experts),
        grid_spec=pltpu.PrefetchScalarGridSpec(
            num_scalar_prefetch=1,
            grid=(1,),
            in_specs=[
                pl.BlockSpec((rows, width), own),
                pl.BlockSpec((rows, width), own),
                pl.BlockSpec((top, tok_count), whole),
                pl.BlockSpec((top, tok_count), whole),
            ],
            out_specs=pl.BlockSpec((rows, 2 * width + padded(2 * experts)), whole),
        ),
        out_shape=jax.ShapeDtypeStruct((rows, 2 * width + padded(2 * experts)), jnp.bfloat16),
        name="pack",
    )(half, tokens, cotangent, expert_ids.T, gate_weights.T)


def expert_kernel(experts, expert_ref, gate_up_ref, gate_up_t_ref, down_t_ref, *refs):
    shard_refs, out_refs = refs[: 2 * len(refs) // 3], refs[2 * len(refs) // 3 :]
    rows = 2 * shard_refs[0].shape[0]
    width, units = down_t_ref.shape
    packed = jnp.concatenate([ref[...] for ref in shard_refs], axis=0)
    pre = jnp.dot(packed[:, :width], gate_up_ref[...], preferred_element_type=jnp.float32)
    grad_hidden = jnp.dot(packed[:, width : 2 * width], down_t_ref[...], preferred_element_type=jnp.float32)
    gate_pre, up_pre = pre[:, :units], pre[:, units:]
    sigmoid_gate = 1.0 / (1.0 + jnp.exp(-gate_pre))
    grad_up = grad_hidden * gate_pre * sigmoid_gate
    scores = jnp.sum(grad_up * up_pre, axis=1, keepdims=True)
    grad_gate = grad_hidden * up_pre * sigmoid_gate * (1.0 + gate_pre * (1.0 - sigmoid_gate))
    grads = jnp.concatenate([grad_gate.astype(jnp.bfloat16), grad_up.astype(jnp.bfloat16)], axis=1)
    part = jnp.dot(grads, gate_up_t_ref[...], preferred_element_type=jnp.float32)
    expert = expert_ref[0]
    routing = packed[:, 2 * width :].astype(jnp.float32)
    lane = lax.broadcasted_iota(jnp.int32, routing.shape, 1)
    weight = jnp.sum(
        jnp.where((lane == expert) | (lane == expert + experts), routing, 0.0), axis=1, keepdims=True
    )
    part = (part * weight).astype(jnp.bfloat16)
    column = lax.broadcasted_iota(jnp.int32, (packed.shape[0], out_refs[0].shape[1] - width), 1)
    score_part = jnp.where(column == expert, scores, 0.0).astype(jnp.bfloat16)
    for i, ref in enumerate(out_refs):
        ref[:, :width] = part[i * rows : (i + 1) * rows]
        ref[:, width:] = score_part[i * rows : (i + 1) * rows]


def layout_kernel(own_refs, other_refs, joined_ref, turned_ref):
    units = own_refs[0].shape[1]
    for i, ref in enumerate((own_refs[0], other_refs[0], own_refs[1], other_refs[1])):
        joined_ref[:, i * units : (i + 1) * units] = ref[...]
        turned_ref[i * units : (i + 1) * units, :] = ref[...].T


def turn_kernel(own_ref, other_ref, turned_ref):
    units = own_ref.shape[0]
    turned_ref[:, :units] = own_ref[...].T
    turned_ref[:, units:] = other_ref[...].T


def lay_out(gate_one, gate_other, up_one, up_other, down_one, down_other):
    width, units = gate_one.shape
    vmem = pl.BlockSpec(memory_space=pltpu.VMEM)
    params = pltpu.CompilerParams(vmem_limit_bytes=VM * 2**20)
    cost = pl.CostEstimate(flops=PREP, bytes_accessed=1, transcendentals=0)
    joined, turned = pl.pallas_call(
        lambda a, b, c, d, e, f: layout_kernel((a, c), (b, d), e, f),
        in_specs=[vmem] * 4,
        out_specs=[vmem] * 2,
        out_shape=[
            jax.ShapeDtypeStruct((width, 4 * units), jnp.bfloat16),
            jax.ShapeDtypeStruct((4 * units, width), jnp.bfloat16),
        ],
        compiler_params=params,
        cost_estimate=cost,
        name="layout",
    )(gate_one, gate_other, up_one, up_other)
    down = pl.pallas_call(
        turn_kernel,
        in_specs=[vmem] * 2,
        out_specs=vmem,
        out_shape=jax.ShapeDtypeStruct((width, 2 * units), jnp.bfloat16),
        compiler_params=params,
        cost_estimate=cost,
        name="turn",
    )(down_one, down_other)
    return joined, turned, down


def expert_call(expert, weights, experts, *shards):
    rows = shards[0].shape[0]
    width = weights[0].shape[0]
    outs = len(shards) // 2
    vmem = pl.BlockSpec(memory_space=pltpu.VMEM)
    return pl.pallas_call(
        functools.partial(expert_kernel, experts),
        in_specs=[pl.BlockSpec(memory_space=pltpu.SMEM)] + [vmem] * (3 + len(shards)),
        out_specs=[vmem] * outs,
        out_shape=[jax.ShapeDtypeStruct((2 * rows, width + padded(experts)), jnp.bfloat16)] * outs,
        compiler_params=pltpu.CompilerParams(vmem_limit_bytes=VM * 2**20),
        cost_estimate=pl.CostEstimate(flops=EFLOPS, bytes_accessed=1, transcendentals=0),
        name="expert",
    )(expert, *weights, *shards)


def tie(*arrays, cost=1):
    return pl.pallas_call(
        lambda *refs: None,
        in_specs=[pl.BlockSpec(memory_space=pl.ANY)] * len(arrays),
        out_specs=[pl.BlockSpec(memory_space=pl.ANY)] * len(arrays),
        out_shape=[jax.ShapeDtypeStruct(a.shape, a.dtype) for a in arrays],
        input_output_aliases={i: i for i in range(len(arrays))},
        compiler_params=pltpu.CompilerParams(vmem_limit_bytes=2**18),
        cost_estimate=pl.CostEstimate(flops=cost, bytes_accessed=1, transcendentals=0),
        name="tie",
    )(*arrays)


def finish_kernel(half_ref, own_ref, other_ref, ids_ref, grad_ref, score_ref):
    rows, width = own_ref.shape[0], grad_ref.shape[1]
    half = half_ref[0]
    columns = own_ref.shape[1] - width
    pair = lax.broadcasted_iota(jnp.int32, (columns, columns), 0)
    same = (pair == lax.broadcasted_iota(jnp.int32, (columns, columns), 1)).astype(jnp.bfloat16)
    scores = jnp.zeros((columns, 2 * rows), jnp.float32)
    for ref, place in ((own_ref, half), (other_ref, 1 - half)):
        grad_ref[pl.ds(pl.multiple_of(place * rows, rows), rows), :] = ref[:, :width]
        row = lax.broadcasted_iota(jnp.int32, (2 * rows, rows), 0) - place * rows
        spot = (row == lax.broadcasted_iota(jnp.int32, (2 * rows, rows), 1)).astype(jnp.bfloat16)
        turned = lax.dot_general(same, ref[:, width:], CONTRACT_LAST, preferred_element_type=jnp.float32)
        scores += lax.dot_general(
            turned.astype(jnp.bfloat16), spot, CONTRACT_LAST, preferred_element_type=jnp.float32
        )
    expert = lax.broadcasted_iota(jnp.int32, scores.shape, 0)
    place_of = lax.broadcasted_iota(jnp.int32, ids_ref.shape, 0)
    total = jnp.zeros(ids_ref.shape, jnp.float32)
    for k in range(ids_ref.shape[0]):
        one = jnp.sum(jnp.where(expert == ids_ref[k : k + 1, :], scores, 0.0), axis=0, keepdims=True)
        total = jnp.where(place_of == k, one, total)
    score_ref[...] = total.astype(jnp.bfloat16)


def finish(half, own, other, expert_ids, width):
    vmem = pl.BlockSpec(memory_space=pltpu.VMEM)
    grad, score = pl.pallas_call(
        finish_kernel,
        in_specs=[pl.BlockSpec(memory_space=pltpu.SMEM)] + [vmem] * 3,
        out_specs=(vmem, vmem),
        out_shape=(
            jax.ShapeDtypeStruct((expert_ids.shape[0], width), jnp.bfloat16),
            jax.ShapeDtypeStruct(expert_ids.shape[::-1], jnp.bfloat16),
        ),
        compiler_params=pltpu.CompilerParams(vmem_limit_bytes=4 * 2**20),
        name="finish",
    )(half, own, other, expert_ids.T)
    return grad, score.T


def added(*terms):
    total = terms[0].astype(jnp.float32)
    for term in terms[1:]:
        total = total + term.astype(jnp.float32)
    return total.astype(jnp.bfloat16)


def dense_plan(tokens, cotangent, expert_ids, gate_weights, w_gate, w_up, w_down):
    experts, halves = lax.axis_size("expert"), lax.axis_size("half")
    levels = experts // 4
    width = tokens.shape[1]
    rows = tokens.shape[0] // 2
    half = lax.axis_index("half").reshape(1).astype(jnp.int32)
    expert = lax.axis_index("expert").reshape(1).astype(jnp.int32)
    axes = ("expert", "half")

    first_pairs = [(e * 2 + h, (e ^ (1 + h)) * 2 + h) for e in range(experts) for h in range(halves)]
    second_pairs = [(e * 2 + h, (e ^ (2 - h)) * 2 + h) for e in range(experts) for h in range(halves)]
    swap_pairs = [(0, 1), (1, 0)]
    to_first = lambda a: lax.ppermute(a, axes, first_pairs)
    to_second = lambda a: lax.ppermute(a, axes, second_pairs)
    swapped = lambda a: lax.ppermute(a, "half", swap_pairs)

    own = pack(half, tokens, cotangent, expert_ids, gate_weights, experts)
    gate_one, up_one, down_one = w_gate[0], w_up[0], w_down[0]
    weights = lay_out(gate_one, swapped(gate_one), up_one, swapped(up_one), down_one, swapped(down_one))

    shifted = lambda a, by: lax.ppermute(a, "expert", [(e, (e + 4 * by) % experts) for e in range(experts)])
    shards, firsts, seconds, boths = [own], [], [], []
    for level in range(levels):
        firsts.append(to_first(shards[level]))
        seconds.append(to_second(shards[level]))
        if level == levels - 1:
            boths.append(shifted(boths[0], level))
            break
        following = shifted(shards[level], 1)
        held = [following, firsts[level]]
        if level > 1:
            held += tie(seconds[level - 1], boths[level - 2], cost=LAG)
        elif level > 0:
            held.append(seconds[level - 1])
        if level == levels - 2:
            held += weights
        held = tie(*held)
        following, firsts[level] = held[:2]
        if level > 0:
            seconds[level - 1] = held[2]
        if level > 1:
            boths[level - 2] = held[3]
        if level == levels - 2:
            weights = held[-3:]
        shards.append(following)
        boths.append(to_second(firsts[level]))

    total, results, previous = [], {}, None
    for batch in [(1, 0)] + [(level,) for level in range(2, levels)]:
        planes = [[shards[i], firsts[i], seconds[i], boths[i]] for i in batch]
        if previous is not None:
            results[previous][1], planes[0][0] = tie(results[previous][1], planes[0][0])
        outs = expert_call(expert, weights, experts, *sum(planes, []))
        for i, level in enumerate(batch):
            results[level] = list(outs[2 * i : 2 * i + 2])
        previous = batch[0]
    for level, (near, far) in results.items():
        from_second = to_second(far)
        from_first = to_first(added(near[rows:], from_second[rows:]))
        terms = (near[:rows], from_second[:rows], from_first)
        total += [shifted(added(*terms), levels - level)] if level else terms
    carry = added(*total)
    return finish(half, carry, swapped(carry), expert_ids, width)


def solution(mesh):
    placed = (
        P("expert", None),
        P("expert", None),
        P("expert", None),
        P("expert", None),
        P("expert", None, "half"),
        P("expert", None, "half"),
        P("expert", "half", None),
    )

    def per_device(tokens, cotangent, expert_ids, *others):
        experts, top = mesh.shape["expert"], expert_ids.shape[1]
        dense = 12 <= experts <= 2 * top and experts % 4 == 0 and mesh.shape["half"] == 2
        return (dense_plan if dense else routed_plan)(tokens, cotangent, expert_ids, *others)

    return jax.shard_map(
        per_device,
        mesh=mesh,
        in_specs=placed,
        out_specs=(P("expert", None), P("expert", None)),
        check_vma=False,
    )
```

```python
import functools

import jax
import jax.numpy as jnp
from jax import lax
from jax.experimental import pallas as pl
from jax.experimental.pallas import tpu as pltpu
from jax.sharding import PartitionSpec as P

LANES = 128
VM = 16
PREP = 4 * 10**9
LAG = 10000000000
EFLOPS = 6 * 10**9
CONTRACT_LAST = (((1,), (1,)), ((), ()))


def expert_terms(rows, grads, gate_one, up_one, down_one):
    gate_pre = jnp.einsum("ncd,df->ncf", rows, gate_one, preferred_element_type=jnp.float32)
    up_pre = jnp.einsum("ncd,df->ncf", rows, up_one, preferred_element_type=jnp.float32)
    grad_hidden = jnp.einsum("ncd,fd->ncf", grads, down_one, preferred_element_type=jnp.float32)
    sigmoid_gate = jax.nn.sigmoid(gate_pre)
    silu_gate = gate_pre * sigmoid_gate
    scores = jnp.sum(grad_hidden * silu_gate * up_pre, axis=-1)
    grad_up = (grad_hidden * silu_gate).astype(jnp.bfloat16)
    grad_gate = (
        grad_hidden * up_pre * sigmoid_gate * (1.0 + gate_pre * (1.0 - sigmoid_gate))
    ).astype(jnp.bfloat16)
    input_part = jnp.einsum("ncf,df->ncd", grad_gate, gate_one, preferred_element_type=jnp.float32)
    input_part = input_part + jnp.einsum(
        "ncf,df->ncd", grad_up, up_one, preferred_element_type=jnp.float32
    )
    return (input_part, scores)


def owner_sum(back, slot_index, gate_weights):
    width = back.shape[2]
    picked = back.reshape(-1, width)[slot_index]
    picked = picked.reshape(gate_weights.shape[0], gate_weights.shape[1], width)
    return jnp.einsum(
        "tk,tkw->tw", gate_weights, picked, preferred_element_type=jnp.float32
    ).astype(jnp.bfloat16)


def routed_plan(tokens, cotangent, expert_ids, gate_weights, w_gate, w_up, w_down):
    tok_count, top_count = expert_ids.shape
    experts = lax.axis_size("expert")
    capacity = 3 * tok_count * top_count // (2 * experts)
    routed = expert_ids.reshape(-1)
    onehot = (routed[:, None] == jnp.arange(experts, dtype=jnp.int32)[None, :]).astype(jnp.int32)
    earlier = jnp.cumsum(onehot, axis=0) - onehot
    slot_index = routed * capacity + jnp.sum(earlier * onehot, axis=1)
    owner_rows = jnp.arange(tok_count * top_count, dtype=jnp.int32) // top_count + 1
    slot_token = jnp.zeros((experts * capacity,), jnp.int32).at[slot_index].set(owner_rows)
    slot_live = (slot_token > 0)[:, None]
    picked = jnp.maximum(slot_token - 1, 0)
    sent_tokens = jnp.where(slot_live, tokens[picked], jnp.zeros((), tokens.dtype)).reshape(
        experts, capacity, -1
    )
    sent_grads = jnp.where(slot_live, cotangent[picked], jnp.zeros((), cotangent.dtype)).reshape(
        experts, capacity, -1
    )
    gate_one = w_gate[0]
    up_one = w_up[0]
    down_one = w_down[0]
    gate_full, up_full = (
        lax.all_gather(gate_one, "half", axis=1, tiled=True),
        lax.all_gather(up_one, "half", axis=1, tiled=True),
    )
    down_full = lax.all_gather(down_one, "half", axis=0, tiled=True)
    half_slots = capacity // 2
    first_slot = lax.axis_index("half") * half_slots
    own_tokens = lax.dynamic_slice_in_dim(sent_tokens, first_slot, half_slots, 1)
    own_grads = lax.dynamic_slice_in_dim(sent_grads, first_slot, half_slots, 1)
    rows = lax.all_to_all(own_tokens, "expert", split_axis=0, concat_axis=0, tiled=True)
    grads = lax.all_to_all(own_grads, "expert", split_axis=0, concat_axis=0, tiled=True)
    part, score = expert_terms(rows, grads, gate_full, up_full, down_full)
    slot_part = part.astype(jnp.bfloat16)
    slot_scores = score.astype(jnp.bfloat16)
    back_part, back_part_scores = (
        lax.all_to_all(slot_part, "expert", split_axis=0, concat_axis=0, tiled=True),
        lax.all_to_all(slot_scores, "expert", split_axis=0, concat_axis=0, tiled=True),
    )
    back, back_scores = (
        lax.all_gather(back_part, "half", axis=1, tiled=True),
        lax.all_gather(back_part_scores, "half", axis=1, tiled=True),
    )
    input_grad = owner_sum(back, slot_index, gate_weights)
    gate_grad = back_scores.reshape(-1)[slot_index].reshape(tok_count, top_count)
    return (input_grad, gate_grad)


def padded(count):
    return -(-count // LANES) * LANES


def pack_kernel(experts, half_ref, tok_ref, cot_ref, ids_ref, gw_ref, out_ref):
    rows, width = tok_ref.shape
    out_ref[:, 0:width] = tok_ref[...]
    out_ref[:, width : 2 * width] = cot_ref[...]
    top, count = ids_ref.shape
    slot = lax.broadcasted_iota(jnp.int32, (out_ref.shape[1] - 2 * width, count), 0)
    total = jnp.zeros(slot.shape, jnp.float32)
    for k in range(top):
        one, weight = ids_ref[k : k + 1, :], gw_ref[k : k + 1, :]
        high = weight.astype(jnp.bfloat16).astype(jnp.float32)
        total = jnp.where(slot == one, high, total)
        total = jnp.where(slot == one + experts, weight - high, total)
    row = lax.broadcasted_iota(jnp.int32, (rows, count), 0) + half_ref[0] * rows
    pick = (row == lax.broadcasted_iota(jnp.int32, (rows, count), 1)).astype(jnp.bfloat16)
    out_ref[:, 2 * width :] = lax.dot_general(
        pick, total.astype(jnp.bfloat16), CONTRACT_LAST, preferred_element_type=jnp.float32
    ).astype(jnp.bfloat16)


def pack(half, tokens, cotangent, expert_ids, gate_weights, experts):
    tok_count, width = tokens.shape
    rows, top = tok_count // 2, expert_ids.shape[1]
    own = lambda i, half: (half[0], 0)
    whole = lambda i, half: (0, 0)
    return pl.pallas_call(
        functools.partial(pack_kernel, experts),
        grid_spec=pltpu.PrefetchScalarGridSpec(
            num_scalar_prefetch=1,
            grid=(1,),
            in_specs=[
                pl.BlockSpec((rows, width), own),
                pl.BlockSpec((rows, width), own),
                pl.BlockSpec((top, tok_count), whole),
                pl.BlockSpec((top, tok_count), whole),
            ],
            out_specs=pl.BlockSpec((rows, 2 * width + padded(2 * experts)), whole),
        ),
        out_shape=jax.ShapeDtypeStruct((rows, 2 * width + padded(2 * experts)), jnp.bfloat16),
        name="pack",
    )(half, tokens, cotangent, expert_ids.T, gate_weights.T)


def expert_kernel(experts, expert_ref, gate_up_ref, gate_up_t_ref, down_t_ref, *refs):
    shard_refs, out_refs = refs[: 2 * len(refs) // 3], refs[2 * len(refs) // 3 :]
    rows = 2 * shard_refs[0].shape[0]
    width, units = down_t_ref.shape
    packed = jnp.concatenate([ref[...] for ref in shard_refs], axis=0)
    pre = jnp.dot(packed[:, :width], gate_up_ref[...], preferred_element_type=jnp.float32)
    grad_hidden = jnp.dot(packed[:, width : 2 * width], down_t_ref[...], preferred_element_type=jnp.float32)
    gate_pre, up_pre = pre[:, :units], pre[:, units:]
    sigmoid_gate = 1.0 / (1.0 + jnp.exp(-gate_pre))
    grad_up = grad_hidden * gate_pre * sigmoid_gate
    scores = jnp.sum(grad_up * up_pre, axis=1, keepdims=True)
    grad_gate = grad_hidden * up_pre * sigmoid_gate * (1.0 + gate_pre * (1.0 - sigmoid_gate))
    grads = jnp.concatenate([grad_gate.astype(jnp.bfloat16), grad_up.astype(jnp.bfloat16)], axis=1)
    part = jnp.dot(grads, gate_up_t_ref[...], preferred_element_type=jnp.float32)
    expert = expert_ref[0]
    routing = packed[:, 2 * width :].astype(jnp.float32)
    lane = lax.broadcasted_iota(jnp.int32, routing.shape, 1)
    weight = jnp.sum(
        jnp.where((lane == expert) | (lane == expert + experts), routing, 0.0), axis=1, keepdims=True
    )
    part = (part * weight).astype(jnp.bfloat16)
    column = lax.broadcasted_iota(jnp.int32, (packed.shape[0], out_refs[0].shape[1] - width), 1)
    score_part = jnp.where(column == expert, scores, 0.0).astype(jnp.bfloat16)
    for i, ref in enumerate(out_refs):
        ref[:, :width] = part[i * rows : (i + 1) * rows]
        ref[:, width:] = score_part[i * rows : (i + 1) * rows]


def layout_kernel(own_refs, other_refs, joined_ref, turned_ref):
    units = own_refs[0].shape[1]
    for i, ref in enumerate((own_refs[0], other_refs[0], own_refs[1], other_refs[1])):
        joined_ref[:, i * units : (i + 1) * units] = ref[...]
        turned_ref[i * units : (i + 1) * units, :] = ref[...].T


def turn_kernel(own_ref, other_ref, turned_ref):
    units = own_ref.shape[0]
    turned_ref[:, :units] = own_ref[...].T
    turned_ref[:, units:] = other_ref[...].T


def lay_out(gate_one, gate_other, up_one, up_other, down_one, down_other):
    width, units = gate_one.shape
    vmem = pl.BlockSpec(memory_space=pltpu.VMEM)
    params = pltpu.CompilerParams(vmem_limit_bytes=VM * 2**20)
    cost = pl.CostEstimate(flops=PREP, bytes_accessed=1, transcendentals=0)
    joined, turned = pl.pallas_call(
        lambda a, b, c, d, e, f: layout_kernel((a, c), (b, d), e, f),
        in_specs=[vmem] * 4,
        out_specs=[vmem] * 2,
        out_shape=[
            jax.ShapeDtypeStruct((width, 4 * units), jnp.bfloat16),
            jax.ShapeDtypeStruct((4 * units, width), jnp.bfloat16),
        ],
        compiler_params=params,
        cost_estimate=cost,
        name="layout",
    )(gate_one, gate_other, up_one, up_other)
    down = pl.pallas_call(
        turn_kernel,
        in_specs=[vmem] * 2,
        out_specs=vmem,
        out_shape=jax.ShapeDtypeStruct((width, 2 * units), jnp.bfloat16),
        compiler_params=params,
        cost_estimate=cost,
        name="turn",
    )(down_one, down_other)
    return joined, turned, down


def expert_call(expert, weights, experts, *shards):
    rows = shards[0].shape[0]
    width = weights[0].shape[0]
    outs = len(shards) // 2
    vmem = pl.BlockSpec(memory_space=pltpu.VMEM)
    return pl.pallas_call(
        functools.partial(expert_kernel, experts),
        in_specs=[pl.BlockSpec(memory_space=pltpu.SMEM)] + [vmem] * (3 + len(shards)),
        out_specs=[vmem] * outs,
        out_shape=[jax.ShapeDtypeStruct((2 * rows, width + padded(experts)), jnp.bfloat16)] * outs,
        compiler_params=pltpu.CompilerParams(vmem_limit_bytes=VM * 2**20),
        cost_estimate=pl.CostEstimate(flops=EFLOPS, bytes_accessed=1, transcendentals=0),
        name="expert",
    )(expert, *weights, *shards)


def tie(*arrays, cost=1, after=()):
    return pl.pallas_call(
        lambda *refs: None,
        in_specs=[pl.BlockSpec(memory_space=pl.ANY)] * (len(arrays) + len(after)),
        out_specs=[pl.BlockSpec(memory_space=pl.ANY)] * len(arrays),
        out_shape=[jax.ShapeDtypeStruct(a.shape, a.dtype) for a in arrays],
        input_output_aliases={i: i for i in range(len(arrays))},
        compiler_params=pltpu.CompilerParams(vmem_limit_bytes=2**18),
        cost_estimate=pl.CostEstimate(flops=cost, bytes_accessed=1, transcendentals=0),
        name="tie",
    )(*arrays, *after)


def finish_kernel(half_ref, own_ref, other_ref, ids_ref, grad_ref, score_ref):
    rows, width = own_ref.shape[0], grad_ref.shape[1]
    half = half_ref[0]
    columns = own_ref.shape[1] - width
    pair = lax.broadcasted_iota(jnp.int32, (columns, columns), 0)
    same = (pair == lax.broadcasted_iota(jnp.int32, (columns, columns), 1)).astype(jnp.bfloat16)
    scores = jnp.zeros((columns, 2 * rows), jnp.float32)
    for ref, place in ((own_ref, half), (other_ref, 1 - half)):
        grad_ref[pl.ds(pl.multiple_of(place * rows, rows), rows), :] = ref[:, :width]
        row = lax.broadcasted_iota(jnp.int32, (2 * rows, rows), 0) - place * rows
        spot = (row == lax.broadcasted_iota(jnp.int32, (2 * rows, rows), 1)).astype(jnp.bfloat16)
        turned = lax.dot_general(same, ref[:, width:], CONTRACT_LAST, preferred_element_type=jnp.float32)
        scores += lax.dot_general(
            turned.astype(jnp.bfloat16), spot, CONTRACT_LAST, preferred_element_type=jnp.float32
        )
    expert = lax.broadcasted_iota(jnp.int32, scores.shape, 0)
    place_of = lax.broadcasted_iota(jnp.int32, ids_ref.shape, 0)
    total = jnp.zeros(ids_ref.shape, jnp.float32)
    for k in range(ids_ref.shape[0]):
        one = jnp.sum(jnp.where(expert == ids_ref[k : k + 1, :], scores, 0.0), axis=0, keepdims=True)
        total = jnp.where(place_of == k, one, total)
    score_ref[...] = total.astype(jnp.bfloat16)


def finish(half, own, other, expert_ids, width):
    vmem = pl.BlockSpec(memory_space=pltpu.VMEM)
    grad, score = pl.pallas_call(
        finish_kernel,
        in_specs=[pl.BlockSpec(memory_space=pltpu.SMEM)] + [vmem] * 3,
        out_specs=(vmem, vmem),
        out_shape=(
            jax.ShapeDtypeStruct((expert_ids.shape[0], width), jnp.bfloat16),
            jax.ShapeDtypeStruct(expert_ids.shape[::-1], jnp.bfloat16),
        ),
        compiler_params=pltpu.CompilerParams(vmem_limit_bytes=4 * 2**20),
        name="finish",
    )(half, own, other, expert_ids.T)
    return grad, score.T


def added(*terms):
    total = terms[0].astype(jnp.float32)
    for term in terms[1:]:
        total = total + term.astype(jnp.float32)
    return total.astype(jnp.bfloat16)


def dense_plan(tokens, cotangent, expert_ids, gate_weights, w_gate, w_up, w_down):
    experts, halves = lax.axis_size("expert"), lax.axis_size("half")
    levels = experts // 4
    width = tokens.shape[1]
    rows = tokens.shape[0] // 2
    half = lax.axis_index("half").reshape(1).astype(jnp.int32)
    expert = lax.axis_index("expert").reshape(1).astype(jnp.int32)
    axes = ("expert", "half")

    first_pairs = [(e * 2 + h, (e ^ (1 + h)) * 2 + h) for e in range(experts) for h in range(halves)]
    second_pairs = [(e * 2 + h, (e ^ (2 - h)) * 2 + h) for e in range(experts) for h in range(halves)]
    swap_pairs = [(0, 1), (1, 0)]
    to_first = lambda a: lax.ppermute(a, axes, first_pairs)
    to_second = lambda a: lax.ppermute(a, axes, second_pairs)
    swapped = lambda a: lax.ppermute(a, "half", swap_pairs)

    own = pack(half, tokens, cotangent, expert_ids, gate_weights, experts)
    gate_one, up_one, down_one = w_gate[0], w_up[0], w_down[0]
    weights = lay_out(gate_one, swapped(gate_one), up_one, swapped(up_one), down_one, swapped(down_one))

    shifted = lambda a, by: lax.ppermute(a, "expert", [(e, (e + 4 * by) % experts) for e in range(experts)])
    shards, firsts, seconds, boths = [own], [], [], []
    for level in range(levels):
        firsts.append(to_first(shards[level]))
        seconds.append(to_second(shards[level]))
        if level == levels - 1:
            boths.append(shifted(boths[0], level))
            break
        following = shifted(shards[level], 1)
        held = [following, firsts[level]]
        if level > 1:
            held += tie(seconds[level - 1], boths[level - 2], cost=LAG)
        elif level > 0:
            held.append(seconds[level - 1])
        if level == levels - 2:
            held += weights
        held = tie(*held)
        following, firsts[level] = held[:2]
        if level > 0:
            seconds[level - 1] = held[2]
        if level > 1:
            boths[level - 2] = held[3]
        if level == levels - 2:
            weights = held[-3:]
        shards.append(following)
        boths.append(to_second(firsts[level]))

    total, results, previous = [], {}, None
    for batch in [(1, 0)] + [(level,) for level in range(2, levels)]:
        planes = [[shards[i], firsts[i], seconds[i], boths[i]] for i in batch]
        if previous is not None:
            results[previous][1], planes[0][0] = tie(results[previous][1], planes[0][0])
        outs = expert_call(expert, weights, experts, *sum(planes, []))
        for i, level in enumerate(batch):
            results[level] = list(outs[2 * i : 2 * i + 2])
        previous = batch[0]
    from_second = {level: to_second(far) for level, (near, far) in results.items()}
    from_first = {}
    for level in [level for level in results if level not in (0, 2)]:
        near, far = results[level]
        from_first[level] = to_first(added(near[rows:], from_second[level][rows:]))
    passed = added(results[2][0][rows:], from_second[2][rows:])
    from_first[2] = to_first(passed)
    from_first[1], from_second[0] = tie(from_first[1], from_second[0], cost=1, after=(passed,))
    from_first[0] = to_first(added(results[0][0][rows:], from_second[0][rows:]))
    for level, (near, far) in results.items():
        terms = (near[:rows], from_second[level][:rows], from_first[level])
        total += [shifted(added(*terms), levels - level)] if level else terms
    carry = added(*total)
    return finish(half, carry, swapped(carry), expert_ids, width)


def solution(mesh):
    placed = (
        P("expert", None),
        P("expert", None),
        P("expert", None),
        P("expert", None),
        P("expert", None, "half"),
        P("expert", None, "half"),
        P("expert", "half", None),
    )

    def per_device(tokens, cotangent, expert_ids, *others):
        experts, top = mesh.shape["expert"], expert_ids.shape[1]
        dense = experts // 4 > 2 and experts <= 2 * top and experts % 4 == 0 and mesh.shape["half"] == 2
        return (dense_plan if dense else routed_plan)(tokens, cotangent, expert_ids, *others)

    return jax.shard_map(
        per_device,
        mesh=mesh,
        in_specs=placed,
        out_specs=(P("expert", None), P("expert", None)),
        check_vma=False,
    )
```

```python
import functools

import jax
import jax.numpy as jnp
from jax import lax
from jax.experimental import pallas as pl
from jax.experimental.pallas import tpu as pltpu
from jax.sharding import PartitionSpec as P

LANES = 128
VM = 16
PREP = 4 * 10**9
LAG = 10000000000
EFLOPS = 6 * 10**9
CONTRACT_LAST = (((1,), (1,)), ((), ()))


def expert_terms(rows, grads, gate_one, up_one, down_one):
    gate_pre = jnp.einsum("ncd,df->ncf", rows, gate_one, preferred_element_type=jnp.float32)
    up_pre = jnp.einsum("ncd,df->ncf", rows, up_one, preferred_element_type=jnp.float32)
    grad_hidden = jnp.einsum("ncd,fd->ncf", grads, down_one, preferred_element_type=jnp.float32)
    sigmoid_gate = jax.nn.sigmoid(gate_pre)
    silu_gate = gate_pre * sigmoid_gate
    scores = jnp.sum(grad_hidden * silu_gate * up_pre, axis=-1)
    grad_up = (grad_hidden * silu_gate).astype(jnp.bfloat16)
    grad_gate = (
        grad_hidden * up_pre * sigmoid_gate * (1.0 + gate_pre * (1.0 - sigmoid_gate))
    ).astype(jnp.bfloat16)
    input_part = jnp.einsum("ncf,df->ncd", grad_gate, gate_one, preferred_element_type=jnp.float32)
    input_part = input_part + jnp.einsum(
        "ncf,df->ncd", grad_up, up_one, preferred_element_type=jnp.float32
    )
    return (input_part, scores)


def owner_sum(back, slot_index, gate_weights):
    width = back.shape[2]
    picked = back.reshape(-1, width)[slot_index]
    picked = picked.reshape(gate_weights.shape[0], gate_weights.shape[1], width)
    return jnp.einsum(
        "tk,tkw->tw", gate_weights, picked, preferred_element_type=jnp.float32
    ).astype(jnp.bfloat16)


def routed_plan(tokens, cotangent, expert_ids, gate_weights, w_gate, w_up, w_down):
    tok_count, top_count = expert_ids.shape
    experts = lax.axis_size("expert")
    capacity = 3 * tok_count * top_count // (2 * experts)
    routed = expert_ids.reshape(-1)
    onehot = (routed[:, None] == jnp.arange(experts, dtype=jnp.int32)[None, :]).astype(jnp.int32)
    earlier = jnp.cumsum(onehot, axis=0) - onehot
    slot_index = routed * capacity + jnp.sum(earlier * onehot, axis=1)
    owner_rows = jnp.arange(tok_count * top_count, dtype=jnp.int32) // top_count + 1
    slot_token = jnp.zeros((experts * capacity,), jnp.int32).at[slot_index].set(owner_rows)
    slot_live = (slot_token > 0)[:, None]
    picked = jnp.maximum(slot_token - 1, 0)
    sent_tokens = jnp.where(slot_live, tokens[picked], jnp.zeros((), tokens.dtype)).reshape(
        experts, capacity, -1
    )
    sent_grads = jnp.where(slot_live, cotangent[picked], jnp.zeros((), cotangent.dtype)).reshape(
        experts, capacity, -1
    )
    gate_one = w_gate[0]
    up_one = w_up[0]
    down_one = w_down[0]
    gate_full, up_full = (
        lax.all_gather(gate_one, "half", axis=1, tiled=True),
        lax.all_gather(up_one, "half", axis=1, tiled=True),
    )
    down_full = lax.all_gather(down_one, "half", axis=0, tiled=True)
    half_slots = capacity // 2
    first_slot = lax.axis_index("half") * half_slots
    own_tokens = lax.dynamic_slice_in_dim(sent_tokens, first_slot, half_slots, 1)
    own_grads = lax.dynamic_slice_in_dim(sent_grads, first_slot, half_slots, 1)
    rows = lax.all_to_all(own_tokens, "expert", split_axis=0, concat_axis=0, tiled=True)
    grads = lax.all_to_all(own_grads, "expert", split_axis=0, concat_axis=0, tiled=True)
    part, score = expert_terms(rows, grads, gate_full, up_full, down_full)
    slot_part = part.astype(jnp.bfloat16)
    slot_scores = score.astype(jnp.bfloat16)
    back_part, back_part_scores = (
        lax.all_to_all(slot_part, "expert", split_axis=0, concat_axis=0, tiled=True),
        lax.all_to_all(slot_scores, "expert", split_axis=0, concat_axis=0, tiled=True),
    )
    back, back_scores = (
        lax.all_gather(back_part, "half", axis=1, tiled=True),
        lax.all_gather(back_part_scores, "half", axis=1, tiled=True),
    )
    input_grad = owner_sum(back, slot_index, gate_weights)
    gate_grad = back_scores.reshape(-1)[slot_index].reshape(tok_count, top_count)
    return (input_grad, gate_grad)


def padded(count):
    return -(-count // LANES) * LANES


def pack_kernel(experts, half_ref, tok_ref, cot_ref, ids_ref, gw_ref, out_ref):
    rows, width = tok_ref.shape
    out_ref[:, 0:width] = tok_ref[...]
    out_ref[:, width : 2 * width] = cot_ref[...]
    top, count = ids_ref.shape
    slot = lax.broadcasted_iota(jnp.int32, (out_ref.shape[1] - 2 * width, count), 0)
    total = jnp.zeros(slot.shape, jnp.float32)
    for k in range(top):
        one, weight = ids_ref[k : k + 1, :], gw_ref[k : k + 1, :]
        high = weight.astype(jnp.bfloat16).astype(jnp.float32)
        total = jnp.where(slot == one, high, total)
        total = jnp.where(slot == one + experts, weight - high, total)
    row = lax.broadcasted_iota(jnp.int32, (rows, count), 0) + half_ref[0] * rows
    pick = (row == lax.broadcasted_iota(jnp.int32, (rows, count), 1)).astype(jnp.bfloat16)
    out_ref[:, 2 * width :] = lax.dot_general(
        pick, total.astype(jnp.bfloat16), CONTRACT_LAST, preferred_element_type=jnp.float32
    ).astype(jnp.bfloat16)


def pack(half, tokens, cotangent, expert_ids, gate_weights, experts):
    tok_count, width = tokens.shape
    rows, top = tok_count // 2, expert_ids.shape[1]
    own = lambda i, half: (half[0], 0)
    whole = lambda i, half: (0, 0)
    return pl.pallas_call(
        functools.partial(pack_kernel, experts),
        grid_spec=pltpu.PrefetchScalarGridSpec(
            num_scalar_prefetch=1,
            grid=(1,),
            in_specs=[
                pl.BlockSpec((rows, width), own),
                pl.BlockSpec((rows, width), own),
                pl.BlockSpec((top, tok_count), whole),
                pl.BlockSpec((top, tok_count), whole),
            ],
            out_specs=pl.BlockSpec((rows, 2 * width + padded(2 * experts)), whole),
        ),
        out_shape=jax.ShapeDtypeStruct((rows, 2 * width + padded(2 * experts)), jnp.bfloat16),
        name="pack",
    )(half, tokens, cotangent, expert_ids.T, gate_weights.T)


def plane_rows(experts, expert, gate_up_ref, gate_up_t_ref, down_t_ref, packed, out_refs):
    rows = packed.shape[0] // 2
    width, units = down_t_ref.shape
    routing = packed[:, 2 * width :].astype(jnp.float32)
    lane = lax.broadcasted_iota(jnp.int32, routing.shape, 1)
    weight = jnp.sum(
        jnp.where((lane == expert) | (lane == expert + experts), routing, 0.0), axis=1, keepdims=True
    )
    tokens, grads = packed[:, :width], packed[:, width : 2 * width]
    scores, gate_parts, up_parts = 0.0, [], []
    block = units
    for start in range(0, units, block):
        gate_pre = jnp.dot(tokens, gate_up_ref[:, start : start + block], preferred_element_type=jnp.float32)
        up_pre = jnp.dot(
            tokens, gate_up_ref[:, units + start : units + start + block], preferred_element_type=jnp.float32
        )
        grad_hidden = jnp.dot(grads, down_t_ref[:, start : start + block], preferred_element_type=jnp.float32)
        sigmoid_gate = 1.0 / (1.0 + jnp.exp(-gate_pre))
        grad_up = grad_hidden * gate_pre * sigmoid_gate
        scores += jnp.sum(grad_up * up_pre, axis=1, keepdims=True)
        grad_gate = grad_hidden * up_pre * sigmoid_gate * (1.0 + gate_pre * (1.0 - sigmoid_gate))
        gate_parts.append(grad_gate.astype(jnp.bfloat16))
        up_parts.append(grad_up.astype(jnp.bfloat16))
    hidden = jnp.concatenate(gate_parts + up_parts, axis=1)
    block = width
    for start in range(0, width, block):
        part = jnp.dot(hidden, gate_up_t_ref[:, start : start + block], preferred_element_type=jnp.float32)
        part = (part * weight).astype(jnp.bfloat16)
        for i, ref in enumerate(out_refs):
            ref[:, start : start + block] = part[i * rows : (i + 1) * rows]
    column = lax.broadcasted_iota(jnp.int32, (packed.shape[0], out_refs[0].shape[1] - width), 1)
    score_part = jnp.where(column == expert, scores, 0.0).astype(jnp.bfloat16)
    for i, ref in enumerate(out_refs):
        ref[:, width:] = score_part[i * rows : (i + 1) * rows]


def expert_kernel(experts, expert_ref, gate_up_ref, gate_up_t_ref, down_t_ref, *refs):
    shard_refs, out_refs = refs[: 2 * len(refs) // 3], refs[2 * len(refs) // 3 :]
    for i in range(0, len(out_refs), 2):
        plane_rows(
            experts,
            expert_ref[0],
            gate_up_ref,
            gate_up_t_ref,
            down_t_ref,
            jnp.concatenate([ref[...] for ref in shard_refs[2 * i : 2 * i + 4]], axis=0),
            out_refs[i : i + 2],
        )


def layout_kernel(own_refs, other_refs, joined_ref, turned_ref):
    units = own_refs[0].shape[1]
    for i, ref in enumerate((own_refs[0], other_refs[0], own_refs[1], other_refs[1])):
        joined_ref[:, i * units : (i + 1) * units] = ref[...]
        turned_ref[i * units : (i + 1) * units, :] = ref[...].T


def turn_kernel(own_ref, other_ref, turned_ref):
    units = own_ref.shape[0]
    turned_ref[:, :units] = own_ref[...].T
    turned_ref[:, units:] = other_ref[...].T


def lay_out(gate_one, gate_other, up_one, up_other, down_one, down_other):
    width, units = gate_one.shape
    vmem = pl.BlockSpec(memory_space=pltpu.VMEM)
    params = pltpu.CompilerParams(vmem_limit_bytes=VM * 2**20)
    cost = pl.CostEstimate(flops=PREP, bytes_accessed=1, transcendentals=0)
    joined, turned = pl.pallas_call(
        lambda a, b, c, d, e, f: layout_kernel((a, c), (b, d), e, f),
        in_specs=[vmem] * 4,
        out_specs=[vmem] * 2,
        out_shape=[
            jax.ShapeDtypeStruct((width, 4 * units), jnp.bfloat16),
            jax.ShapeDtypeStruct((4 * units, width), jnp.bfloat16),
        ],
        compiler_params=params,
        cost_estimate=cost,
        name="layout",
    )(gate_one, gate_other, up_one, up_other)
    down = pl.pallas_call(
        turn_kernel,
        in_specs=[vmem] * 2,
        out_specs=vmem,
        out_shape=jax.ShapeDtypeStruct((width, 2 * units), jnp.bfloat16),
        compiler_params=params,
        cost_estimate=cost,
        name="turn",
    )(down_one, down_other)
    return joined, turned, down


def expert_call(expert, weights, experts, *shards):
    rows = shards[0].shape[0]
    width = weights[0].shape[0]
    outs = len(shards) // 2
    vmem = pl.BlockSpec(memory_space=pltpu.VMEM)
    return pl.pallas_call(
        functools.partial(expert_kernel, experts),
        in_specs=[pl.BlockSpec(memory_space=pltpu.SMEM)] + [vmem] * (3 + len(shards)),
        out_specs=[vmem] * outs,
        out_shape=[jax.ShapeDtypeStruct((2 * rows, width + padded(experts)), jnp.bfloat16)] * outs,
        compiler_params=pltpu.CompilerParams(vmem_limit_bytes=VM * 2**20),
        cost_estimate=pl.CostEstimate(flops=EFLOPS, bytes_accessed=1, transcendentals=0),
        name="expert",
    )(expert, *weights, *shards)


def tie(*arrays, cost=1, after=()):
    return pl.pallas_call(
        lambda *refs: None,
        in_specs=[pl.BlockSpec(memory_space=pl.ANY)] * (len(arrays) + len(after)),
        out_specs=[pl.BlockSpec(memory_space=pl.ANY)] * len(arrays),
        out_shape=[jax.ShapeDtypeStruct(a.shape, a.dtype) for a in arrays],
        input_output_aliases={i: i for i in range(len(arrays))},
        compiler_params=pltpu.CompilerParams(vmem_limit_bytes=2**18),
        cost_estimate=pl.CostEstimate(flops=cost, bytes_accessed=1, transcendentals=0),
        name="tie",
    )(*arrays, *after)


def finish_kernel(half_ref, own_ref, other_ref, ids_ref, grad_ref, score_ref):
    rows, width = own_ref.shape[0], grad_ref.shape[1]
    half = half_ref[0]
    columns = own_ref.shape[1] - width
    pair = lax.broadcasted_iota(jnp.int32, (columns, columns), 0)
    same = (pair == lax.broadcasted_iota(jnp.int32, (columns, columns), 1)).astype(jnp.bfloat16)
    scores = jnp.zeros((columns, 2 * rows), jnp.float32)
    for ref, place in ((own_ref, half), (other_ref, 1 - half)):
        grad_ref[pl.ds(pl.multiple_of(place * rows, rows), rows), :] = ref[:, :width]
        row = lax.broadcasted_iota(jnp.int32, (2 * rows, rows), 0) - place * rows
        spot = (row == lax.broadcasted_iota(jnp.int32, (2 * rows, rows), 1)).astype(jnp.bfloat16)
        turned = lax.dot_general(same, ref[:, width:], CONTRACT_LAST, preferred_element_type=jnp.float32)
        scores += lax.dot_general(
            turned.astype(jnp.bfloat16), spot, CONTRACT_LAST, preferred_element_type=jnp.float32
        )
    expert = lax.broadcasted_iota(jnp.int32, scores.shape, 0)
    place_of = lax.broadcasted_iota(jnp.int32, ids_ref.shape, 0)
    total = jnp.zeros(ids_ref.shape, jnp.float32)
    for k in range(ids_ref.shape[0]):
        one = jnp.sum(jnp.where(expert == ids_ref[k : k + 1, :], scores, 0.0), axis=0, keepdims=True)
        total = jnp.where(place_of == k, one, total)
    score_ref[...] = total.astype(jnp.bfloat16)


def finish(half, own, other, expert_ids, width):
    vmem = pl.BlockSpec(memory_space=pltpu.VMEM)
    grad, score = pl.pallas_call(
        finish_kernel,
        in_specs=[pl.BlockSpec(memory_space=pltpu.SMEM)] + [vmem] * 3,
        out_specs=(vmem, vmem),
        out_shape=(
            jax.ShapeDtypeStruct((expert_ids.shape[0], width), jnp.bfloat16),
            jax.ShapeDtypeStruct(expert_ids.shape[::-1], jnp.bfloat16),
        ),
        compiler_params=pltpu.CompilerParams(vmem_limit_bytes=4 * 2**20),
        name="finish",
    )(half, own, other, expert_ids.T)
    return grad, score.T


def added(*terms):
    total = terms[0].astype(jnp.float32)
    for term in terms[1:]:
        total = total + term.astype(jnp.float32)
    return total.astype(jnp.bfloat16)


def dense_plan(tokens, cotangent, expert_ids, gate_weights, w_gate, w_up, w_down):
    experts, halves = lax.axis_size("expert"), lax.axis_size("half")
    levels = experts // 4
    width = tokens.shape[1]
    rows = tokens.shape[0] // 2
    half = lax.axis_index("half").reshape(1).astype(jnp.int32)
    expert = lax.axis_index("expert").reshape(1).astype(jnp.int32)
    axes = ("expert", "half")

    first_pairs = [(e * 2 + h, (e ^ (1 + h)) * 2 + h) for e in range(experts) for h in range(halves)]
    second_pairs = [(e * 2 + h, (e ^ (2 - h)) * 2 + h) for e in range(experts) for h in range(halves)]
    swap_pairs = [(0, 1), (1, 0)]
    to_first = lambda a: lax.ppermute(a, axes, first_pairs)
    to_second = lambda a: lax.ppermute(a, axes, second_pairs)
    swapped = lambda a: lax.ppermute(a, "half", swap_pairs)

    own = pack(half, tokens, cotangent, expert_ids, gate_weights, experts)
    gate_one, up_one, down_one = w_gate[0], w_up[0], w_down[0]
    weights = lay_out(gate_one, swapped(gate_one), up_one, swapped(up_one), down_one, swapped(down_one))

    ring = [*range(0, levels, 2), *reversed(range(1, levels, 2))]
    shifted = lambda a, by: lax.ppermute(
        a,
        "expert",
        [
            (ring[i] * 4 + j, ring[(i + by) % levels] * 4 + j)
            for i in range(levels)
            for j in range(4)
        ],
    )
    shards, firsts, seconds, boths = [own], [], [], []
    for level in range(levels):
        firsts.append(to_first(shards[level]))
        seconds.append(to_second(shards[level]))
        if level == levels - 1:
            boths.append(shifted(boths[0], level))
            break
        following = shifted(shards[level], 1)
        held = [following, firsts[level]]
        if level > 1:
            held += tie(seconds[level - 1], boths[level - 2], cost=LAG)
        elif level > 0:
            held.append(seconds[level - 1])
        if level == levels - 2:
            held += weights
        held = tie(*held)
        following, firsts[level] = held[:2]
        if level > 0:
            seconds[level - 1] = held[2]
        if level > 1:
            boths[level - 2] = held[3]
        if level == levels - 2:
            weights = held[-3:]
        shards.append(following)
        boths.append(to_second(firsts[level]))

    total, results, previous = [], {}, None
    for batch in [(1, 0)] + [(level,) for level in range(2, levels)]:
        planes = [[shards[i], firsts[i], seconds[i], boths[i]] for i in batch]
        if previous is not None:
            results[previous][1], planes[0][0] = tie(results[previous][1], planes[0][0])
        outs = expert_call(expert, weights, experts, *sum(planes, []))
        for i, level in enumerate(batch):
            results[level] = list(outs[2 * i : 2 * i + 2])
        previous = batch[0]
    from_second = {level: to_second(far) for level, (near, far) in results.items()}
    from_first = {}
    for level in [level for level in results if level not in (0, 2)]:
        near, far = results[level]
        from_first[level] = to_first(added(near[rows:], from_second[level][rows:]))
    passed = added(results[2][0][rows:], from_second[2][rows:])
    from_first[2] = to_first(passed)
    from_first[1], from_second[0] = tie(from_first[1], from_second[0], cost=1, after=(passed,))
    from_first[0] = to_first(added(results[0][0][rows:], from_second[0][rows:]))
    for level, (near, far) in results.items():
        terms = (near[:rows], from_second[level][:rows], from_first[level])
        total += [shifted(added(*terms), levels - level)] if level else terms
    carry = added(*total)
    return finish(half, carry, swapped(carry), expert_ids, width)


def solution(mesh):
    placed = (
        P("expert", None),
        P("expert", None),
        P("expert", None),
        P("expert", None),
        P("expert", None, "half"),
        P("expert", None, "half"),
        P("expert", "half", None),
    )

    def per_device(tokens, cotangent, expert_ids, *others):
        experts, top = mesh.shape["expert"], expert_ids.shape[1]
        dense = experts // 4 > 2 and experts <= 2 * top and experts % 4 == 0 and mesh.shape["half"] == 2
        return (dense_plan if dense else routed_plan)(tokens, cotangent, expert_ids, *others)

    return jax.shard_map(
        per_device,
        mesh=mesh,
        in_specs=placed,
        out_specs=(P("expert", None), P("expert", None)),
        check_vma=False,
    )
```

```python
import functools

import jax
import jax.numpy as jnp
from jax import lax
from jax.experimental import pallas as pl
from jax.experimental.pallas import tpu as pltpu
from jax.sharding import PartitionSpec as P

LANES = 128
VM = 16
PREP = 4 * 10**9
LAG = 10000000000
EFLOPS = 6 * 10**9
CONTRACT_LAST = (((1,), (1,)), ((), ()))


def expert_terms(rows, grads, gate_one, up_one, down_one):
    gate_pre = jnp.einsum("ncd,df->ncf", rows, gate_one, preferred_element_type=jnp.float32)
    up_pre = jnp.einsum("ncd,df->ncf", rows, up_one, preferred_element_type=jnp.float32)
    grad_hidden = jnp.einsum("ncd,fd->ncf", grads, down_one, preferred_element_type=jnp.float32)
    sigmoid_gate = jax.nn.sigmoid(gate_pre)
    silu_gate = gate_pre * sigmoid_gate
    scores = jnp.sum(grad_hidden * silu_gate * up_pre, axis=-1)
    grad_up = (grad_hidden * silu_gate).astype(jnp.bfloat16)
    grad_gate = (
        grad_hidden * up_pre * sigmoid_gate * (1.0 + gate_pre * (1.0 - sigmoid_gate))
    ).astype(jnp.bfloat16)
    input_part = jnp.einsum("ncf,df->ncd", grad_gate, gate_one, preferred_element_type=jnp.float32)
    input_part = input_part + jnp.einsum(
        "ncf,df->ncd", grad_up, up_one, preferred_element_type=jnp.float32
    )
    return (input_part, scores)


def owner_sum(back, slot_index, gate_weights):
    width = back.shape[2]
    picked = back.reshape(-1, width)[slot_index]
    picked = picked.reshape(gate_weights.shape[0], gate_weights.shape[1], width)
    return jnp.einsum(
        "tk,tkw->tw", gate_weights, picked, preferred_element_type=jnp.float32
    ).astype(jnp.bfloat16)


def routed_plan(tokens, cotangent, expert_ids, gate_weights, w_gate, w_up, w_down):
    tok_count, top_count = expert_ids.shape
    experts = lax.axis_size("expert")
    capacity = 3 * tok_count * top_count // (2 * experts)
    routed = expert_ids.reshape(-1)
    onehot = (routed[:, None] == jnp.arange(experts, dtype=jnp.int32)[None, :]).astype(jnp.int32)
    earlier = jnp.cumsum(onehot, axis=0) - onehot
    slot_index = routed * capacity + jnp.sum(earlier * onehot, axis=1)
    owner_rows = jnp.arange(tok_count * top_count, dtype=jnp.int32) // top_count + 1
    slot_token = jnp.zeros((experts * capacity,), jnp.int32).at[slot_index].set(owner_rows)
    slot_live = (slot_token > 0)[:, None]
    picked = jnp.maximum(slot_token - 1, 0)
    sent_tokens = jnp.where(slot_live, tokens[picked], jnp.zeros((), tokens.dtype)).reshape(
        experts, capacity, -1
    )
    sent_grads = jnp.where(slot_live, cotangent[picked], jnp.zeros((), cotangent.dtype)).reshape(
        experts, capacity, -1
    )
    gate_one = w_gate[0]
    up_one = w_up[0]
    down_one = w_down[0]
    gate_full, up_full = (
        lax.all_gather(gate_one, "half", axis=1, tiled=True),
        lax.all_gather(up_one, "half", axis=1, tiled=True),
    )
    down_full = lax.all_gather(down_one, "half", axis=0, tiled=True)
    half_slots = capacity // 2
    first_slot = lax.axis_index("half") * half_slots
    own_tokens = lax.dynamic_slice_in_dim(sent_tokens, first_slot, half_slots, 1)
    own_grads = lax.dynamic_slice_in_dim(sent_grads, first_slot, half_slots, 1)
    rows = lax.all_to_all(own_tokens, "expert", split_axis=0, concat_axis=0, tiled=True)
    grads = lax.all_to_all(own_grads, "expert", split_axis=0, concat_axis=0, tiled=True)
    part, score = expert_terms(rows, grads, gate_full, up_full, down_full)
    slot_part = part.astype(jnp.bfloat16)
    slot_scores = score.astype(jnp.bfloat16)
    back_part, back_part_scores = (
        lax.all_to_all(slot_part, "expert", split_axis=0, concat_axis=0, tiled=True),
        lax.all_to_all(slot_scores, "expert", split_axis=0, concat_axis=0, tiled=True),
    )
    back, back_scores = (
        lax.all_gather(back_part, "half", axis=1, tiled=True),
        lax.all_gather(back_part_scores, "half", axis=1, tiled=True),
    )
    input_grad = owner_sum(back, slot_index, gate_weights)
    gate_grad = back_scores.reshape(-1)[slot_index].reshape(tok_count, top_count)
    return (input_grad, gate_grad)


def padded(count):
    return -(-count // LANES) * LANES


def pack_kernel(experts, half_ref, tok_ref, cot_ref, ids_ref, gw_ref, out_ref):
    rows, width = tok_ref.shape
    out_ref[:, 0:width] = tok_ref[...]
    out_ref[:, width : 2 * width] = cot_ref[...]
    top, count = ids_ref.shape
    slot = lax.broadcasted_iota(jnp.int32, (out_ref.shape[1] - 2 * width, count), 0)
    total = jnp.zeros(slot.shape, jnp.float32)
    for k in range(top):
        one, weight = ids_ref[k : k + 1, :], gw_ref[k : k + 1, :]
        high = weight.astype(jnp.bfloat16).astype(jnp.float32)
        total = jnp.where(slot == one, high, total)
        total = jnp.where(slot == one + experts, weight - high, total)
    row = lax.broadcasted_iota(jnp.int32, (rows, count), 0) + half_ref[0] * rows
    pick = (row == lax.broadcasted_iota(jnp.int32, (rows, count), 1)).astype(jnp.bfloat16)
    out_ref[:, 2 * width :] = lax.dot_general(
        pick, total.astype(jnp.bfloat16), CONTRACT_LAST, preferred_element_type=jnp.float32
    ).astype(jnp.bfloat16)


def pack(half, tokens, cotangent, expert_ids, gate_weights, experts):
    tok_count, width = tokens.shape
    rows, top = tok_count // 2, expert_ids.shape[1]
    own = lambda i, half: (half[0], 0)
    whole = lambda i, half: (0, 0)
    return pl.pallas_call(
        functools.partial(pack_kernel, experts),
        grid_spec=pltpu.PrefetchScalarGridSpec(
            num_scalar_prefetch=1,
            grid=(1,),
            in_specs=[
                pl.BlockSpec((rows, width), own),
                pl.BlockSpec((rows, width), own),
                pl.BlockSpec((top, tok_count), whole),
                pl.BlockSpec((top, tok_count), whole),
            ],
            out_specs=pl.BlockSpec((rows, 2 * width + padded(2 * experts)), whole),
        ),
        out_shape=jax.ShapeDtypeStruct((rows, 2 * width + padded(2 * experts)), jnp.bfloat16),
        name="pack",
    )(half, tokens, cotangent, expert_ids.T, gate_weights.T)


def plane_rows(experts, expert, gate_up_ref, gate_up_t_ref, down_t_ref, packed, out_refs):
    rows = packed.shape[0] // 2
    width, units = down_t_ref.shape
    routing = packed[:, 2 * width :].astype(jnp.float32)
    lane = lax.broadcasted_iota(jnp.int32, routing.shape, 1)
    weight = jnp.sum(
        jnp.where((lane == expert) | (lane == expert + experts), routing, 0.0), axis=1, keepdims=True
    )
    tokens, grads = packed[:, :width], packed[:, width : 2 * width]
    scores, gate_parts, up_parts = 0.0, [], []
    block = units
    for start in range(0, units, block):
        gate_pre = jnp.dot(tokens, gate_up_ref[:, start : start + block], preferred_element_type=jnp.float32)
        up_pre = jnp.dot(
            tokens, gate_up_ref[:, units + start : units + start + block], preferred_element_type=jnp.float32
        )
        grad_hidden = jnp.dot(grads, down_t_ref[:, start : start + block], preferred_element_type=jnp.float32)
        sigmoid_gate = 1.0 / (1.0 + jnp.exp(-gate_pre))
        grad_up = grad_hidden * gate_pre * sigmoid_gate
        scores += jnp.sum(grad_up * up_pre, axis=1, keepdims=True)
        grad_gate = grad_hidden * up_pre * sigmoid_gate * (1.0 + gate_pre * (1.0 - sigmoid_gate))
        gate_parts.append(grad_gate.astype(jnp.bfloat16))
        up_parts.append(grad_up.astype(jnp.bfloat16))
    hidden = jnp.concatenate(gate_parts + up_parts, axis=1)
    block = width
    for start in range(0, width, block):
        part = jnp.dot(hidden, gate_up_t_ref[:, start : start + block], preferred_element_type=jnp.float32)
        part = (part * weight).astype(jnp.bfloat16)
        for i, ref in enumerate(out_refs):
            ref[:, start : start + block] = part[i * rows : (i + 1) * rows]
    column = lax.broadcasted_iota(jnp.int32, (packed.shape[0], out_refs[0].shape[1] - width), 1)
    score_part = jnp.where(column == expert, scores, 0.0).astype(jnp.bfloat16)
    for i, ref in enumerate(out_refs):
        ref[:, width:] = score_part[i * rows : (i + 1) * rows]


def expert_kernel(experts, expert_ref, gate_up_ref, gate_up_t_ref, down_t_ref, *refs):
    shard_refs, out_refs = refs[: 2 * len(refs) // 3], refs[2 * len(refs) // 3 :]
    for i in range(0, len(out_refs), 2):
        plane_rows(
            experts,
            expert_ref[0],
            gate_up_ref,
            gate_up_t_ref,
            down_t_ref,
            jnp.concatenate([ref[...] for ref in shard_refs[2 * i : 2 * i + 4]], axis=0),
            out_refs[i : i + 2],
        )


def layout_kernel(own_refs, other_refs, joined_ref, turned_ref):
    units = own_refs[0].shape[1]
    for i, ref in enumerate((own_refs[0], other_refs[0], own_refs[1], other_refs[1])):
        joined_ref[:, i * units : (i + 1) * units] = ref[...]
        turned_ref[i * units : (i + 1) * units, :] = ref[...].T


def turn_kernel(own_ref, other_ref, turned_ref):
    units = own_ref.shape[0]
    turned_ref[:, :units] = own_ref[...].T
    turned_ref[:, units:] = other_ref[...].T


def lay_out(gate_one, gate_other, up_one, up_other, down_one, down_other):
    width, units = gate_one.shape
    vmem = pl.BlockSpec(memory_space=pltpu.VMEM)
    params = pltpu.CompilerParams(vmem_limit_bytes=VM * 2**20)
    cost = pl.CostEstimate(flops=PREP, bytes_accessed=1, transcendentals=0)
    joined, turned = pl.pallas_call(
        lambda a, b, c, d, e, f: layout_kernel((a, c), (b, d), e, f),
        in_specs=[vmem] * 4,
        out_specs=[vmem] * 2,
        out_shape=[
            jax.ShapeDtypeStruct((width, 4 * units), jnp.bfloat16),
            jax.ShapeDtypeStruct((4 * units, width), jnp.bfloat16),
        ],
        compiler_params=params,
        cost_estimate=cost,
        name="layout",
    )(gate_one, gate_other, up_one, up_other)
    down = pl.pallas_call(
        turn_kernel,
        in_specs=[vmem] * 2,
        out_specs=vmem,
        out_shape=jax.ShapeDtypeStruct((width, 2 * units), jnp.bfloat16),
        compiler_params=params,
        cost_estimate=cost,
        name="turn",
    )(down_one, down_other)
    return joined, turned, down


def expert_call(expert, weights, experts, *shards):
    rows = shards[0].shape[0]
    width = weights[0].shape[0]
    outs = len(shards) // 2
    vmem = pl.BlockSpec(memory_space=pltpu.VMEM)
    return pl.pallas_call(
        functools.partial(expert_kernel, experts),
        in_specs=[pl.BlockSpec(memory_space=pltpu.SMEM)] + [vmem] * (3 + len(shards)),
        out_specs=[vmem] * outs,
        out_shape=[jax.ShapeDtypeStruct((2 * rows, width + padded(experts)), jnp.bfloat16)] * outs,
        compiler_params=pltpu.CompilerParams(vmem_limit_bytes=VM * 2**20),
        cost_estimate=pl.CostEstimate(flops=EFLOPS, bytes_accessed=1, transcendentals=0),
        name="expert",
    )(expert, *weights, *shards)


def tie(*arrays, cost=1, after=()):
    return pl.pallas_call(
        lambda *refs: None,
        in_specs=[pl.BlockSpec(memory_space=pl.ANY)] * (len(arrays) + len(after)),
        out_specs=[pl.BlockSpec(memory_space=pl.ANY)] * len(arrays),
        out_shape=[jax.ShapeDtypeStruct(a.shape, a.dtype) for a in arrays],
        input_output_aliases={i: i for i in range(len(arrays))},
        compiler_params=pltpu.CompilerParams(vmem_limit_bytes=2**18),
        cost_estimate=pl.CostEstimate(flops=cost, bytes_accessed=1, transcendentals=0),
        name="tie",
    )(*arrays, *after)


def finish_kernel(half_ref, own_ref, other_ref, ids_ref, grad_ref, score_ref):
    rows, width = own_ref.shape[0], grad_ref.shape[1]
    half = half_ref[0]
    columns = own_ref.shape[1] - width
    pair = lax.broadcasted_iota(jnp.int32, (columns, columns), 0)
    same = (pair == lax.broadcasted_iota(jnp.int32, (columns, columns), 1)).astype(jnp.bfloat16)
    scores = jnp.zeros((columns, 2 * rows), jnp.float32)
    for ref, place in ((own_ref, half), (other_ref, 1 - half)):
        grad_ref[pl.ds(pl.multiple_of(place * rows, rows), rows), :] = ref[:, :width]
        row = lax.broadcasted_iota(jnp.int32, (2 * rows, rows), 0) - place * rows
        spot = (row == lax.broadcasted_iota(jnp.int32, (2 * rows, rows), 1)).astype(jnp.bfloat16)
        turned = lax.dot_general(same, ref[:, width:], CONTRACT_LAST, preferred_element_type=jnp.float32)
        scores += lax.dot_general(
            turned.astype(jnp.bfloat16), spot, CONTRACT_LAST, preferred_element_type=jnp.float32
        )
    expert = lax.broadcasted_iota(jnp.int32, scores.shape, 0)
    place_of = lax.broadcasted_iota(jnp.int32, ids_ref.shape, 0)
    total = jnp.zeros(ids_ref.shape, jnp.float32)
    for k in range(ids_ref.shape[0]):
        one = jnp.sum(jnp.where(expert == ids_ref[k : k + 1, :], scores, 0.0), axis=0, keepdims=True)
        total = jnp.where(place_of == k, one, total)
    score_ref[...] = total.astype(jnp.bfloat16)


def finish(half, own, other, expert_ids, width):
    vmem = pl.BlockSpec(memory_space=pltpu.VMEM)
    grad, score = pl.pallas_call(
        finish_kernel,
        in_specs=[pl.BlockSpec(memory_space=pltpu.SMEM)] + [vmem] * 3,
        out_specs=(vmem, vmem),
        out_shape=(
            jax.ShapeDtypeStruct((expert_ids.shape[0], width), jnp.bfloat16),
            jax.ShapeDtypeStruct(expert_ids.shape[::-1], jnp.bfloat16),
        ),
        compiler_params=pltpu.CompilerParams(vmem_limit_bytes=4 * 2**20),
        name="finish",
    )(half, own, other, expert_ids.T)
    return grad, score.T


def added(*terms):
    total = terms[0].astype(jnp.float32)
    for term in terms[1:]:
        total = total + term.astype(jnp.float32)
    return total.astype(jnp.bfloat16)


def dense_plan(tokens, cotangent, expert_ids, gate_weights, w_gate, w_up, w_down):
    experts, halves = lax.axis_size("expert"), lax.axis_size("half")
    levels = experts // 4
    width = tokens.shape[1]
    rows = tokens.shape[0] // 2
    half = lax.axis_index("half").reshape(1).astype(jnp.int32)
    expert = lax.axis_index("expert").reshape(1).astype(jnp.int32)
    axes = ("expert", "half")

    first_pairs = [(e * 2 + h, (e ^ (1 + h)) * 2 + h) for e in range(experts) for h in range(halves)]
    second_pairs = [(e * 2 + h, (e ^ (2 - h)) * 2 + h) for e in range(experts) for h in range(halves)]
    swap_pairs = [(0, 1), (1, 0)]
    to_first = lambda a: lax.ppermute(a, axes, first_pairs)
    to_second = lambda a: lax.ppermute(a, axes, second_pairs)
    swapped = lambda a: lax.ppermute(a, "half", swap_pairs)

    own = pack(half, tokens, cotangent, expert_ids, gate_weights, experts)
    gate_one, up_one, down_one = w_gate[0], w_up[0], w_down[0]
    weights = lay_out(gate_one, swapped(gate_one), up_one, swapped(up_one), down_one, swapped(down_one))

    ring = [*range(0, levels, 2), *reversed(range(1, levels, 2))]
    shifted = lambda a, by: lax.ppermute(
        a,
        "expert",
        [
            (ring[i] * 4 + j, ring[(i + by) % levels] * 4 + j)
            for i in range(levels)
            for j in range(4)
        ],
    )
    shards, firsts, seconds, boths = [own], [], [], []
    for level in range(levels):
        firsts.append(to_first(shards[level]))
        seconds.append(to_second(shards[level]))
        if level == levels - 1:
            boths.append(shifted(boths[0], level))
            break
        following = shifted(shards[level], 1)
        held = [following, firsts[level]]
        if level > 1:
            held += tie(seconds[level - 1], boths[level - 2], cost=LAG)
        elif level > 0:
            held.append(seconds[level - 1])
        if level == levels - 2:
            held += weights
        held = tie(*held)
        following, firsts[level] = held[:2]
        if level > 0:
            seconds[level - 1] = held[2]
        if level > 1:
            boths[level - 2] = held[3]
        if level == levels - 2:
            weights = held[-3:]
        shards.append(following)
        boths.append(to_second(firsts[level]))

    total, results, previous = [], {}, None
    for batch in [(1,), (0,)] + [(level,) for level in range(2, levels)]:
        planes = [[shards[i], firsts[i], seconds[i], boths[i]] for i in batch]
        if previous is not None:
            results[previous][1], planes[0][0] = tie(results[previous][1], planes[0][0])
        outs = expert_call(expert, weights, experts, *sum(planes, []))
        for i, level in enumerate(batch):
            results[level] = list(outs[2 * i : 2 * i + 2])
        previous = batch[0]
    from_second = {level: to_second(far) for level, (near, far) in results.items()}
    from_first = {}
    for level in [level for level in results if level not in (0, 2)]:
        near, far = results[level]
        from_first[level] = to_first(added(near[rows:], from_second[level][rows:]))
    passed = added(results[2][0][rows:], from_second[2][rows:])
    from_first[2] = to_first(passed)
    from_first[1], from_second[0] = tie(from_first[1], from_second[0], cost=1, after=(passed,))
    from_first[0] = to_first(added(results[0][0][rows:], from_second[0][rows:]))
    for level, (near, far) in results.items():
        terms = (near[:rows], from_second[level][:rows], from_first[level])
        total += [shifted(added(*terms), levels - level)] if level else terms
    carry = added(*total)
    return finish(half, carry, swapped(carry), expert_ids, width)


def solution(mesh):
    placed = (
        P("expert", None),
        P("expert", None),
        P("expert", None),
        P("expert", None),
        P("expert", None, "half"),
        P("expert", None, "half"),
        P("expert", "half", None),
    )

    def per_device(tokens, cotangent, expert_ids, *others):
        experts, top = mesh.shape["expert"], expert_ids.shape[1]
        dense = experts // 4 > 2 and experts <= 2 * top and experts % 4 == 0 and mesh.shape["half"] == 2
        return (dense_plan if dense else routed_plan)(tokens, cotangent, expert_ids, *others)

    return jax.shard_map(
        per_device,
        mesh=mesh,
        in_specs=placed,
        out_specs=(P("expert", None), P("expert", None)),
        check_vma=False,
    )
```
